512 devices in a mesh: sta: 128 (over y, z, core), win: 4 (over x).
Axes of the slice: x: 4, y: 8, z: 8, core: 2. Of those that a mesh axis runs over, the one named last changes fastest.
Arguments:
- spectra: bfloat16 [256, 4, 2, 2048], P('sta', 'win'), may hold values from -6 to 6
- masks: int32 [256, 4], P('sta'), may hold values 0 or 1
- pairs: int32 [16384, 2], P('sta'), may hold values from 0 to 255
- owners: int32 [16384, 1], P('sta'), may hold values from 0 to 127; in each aligned block of 128 rows (0 to 127, 128 to 255, ...) at most 2 rows name the same one
Outputs:
- stacks: float32 [32768, 512], P('sta', 'win')
The draws below stay inside these ranges and needn't reach their ends.
Inputs may be any that keep to these rules, and one draw needn't show every extreme that they name: `owners`: within each aligned block of 128 rows no owner is named more than 2 times, a bound that some block reaches.
All inputs are finite; a program needn't handle non-finite values. No bound on the sum of `masks` on one device may be relied on, other than what follows from the above.
Results may differ from the reference program's by a relative error of at most 0.0023.
Values may be sent and summed in bfloat16 or wider, within the bound.
A program may use at most 64 MiB of HBM per device.

```python
import math
import jax
import jax.numpy as jnp
import numpy as np
from jax import lax

PAIR_DEV = 128
F = 2048
LAGS = 512
FIRST_BIN = 360
SAMPLES = 180000
STATIONS = 256
WINDOWS = 4
PAIRS = 16384
CAP = 2
SLOTS = 256
OUT_ROWS = 32768
N_STA = 128


def with_ends(array, stream_key, low, top_value):
    longest = array.shape.index(max(array.shape))
    spots = []
    for shift in (0, 1):
        where = [jax.random.randint(jax.random.fold_in(stream_key, axis), (), 0, length) for axis, length in enumerate(array.shape)]
        where[longest] = (where[longest] + shift) % array.shape[longest]
        spots.append(tuple(where))
    return array.at[spots[0]].set(low).at[spots[1]].set(top_value)


def block_scale(key, shape, cuts, smallest, top_value):
    def one(dim, blocks):
        draws = jax.random.uniform(jax.random.fold_in(jax.random.fold_in(key, 6), dim), (blocks,), jnp.float32, smallest / len(cuts), top_value / len(cuts))
        return jnp.repeat(jnp.exp(draws), shape[dim] // blocks).reshape((-1,) + (1,) * (len(shape) - dim - 1))

    factor_of = one(*cuts[0])
    for cut in cuts[1:]:
        factor_of = factor_of * one(*cut)
    return factor_of


def assign_block(key, own, number, rows, number_of, top, limit, skew):
    order = jax.random.permutation(key, number_of)
    crowded, common = shares(number_of, rows * top, limit, skew, True), shares(number_of, rows * top, limit, skew, False)
    places = jnp.arange(number_of)

    def named(lengths, rotation):
        used = int((lengths > 0).sum())
        fixed = max(1, used // 4)
        shifted = fixed + (places - fixed + rotation * (used - fixed)) % max(1, number_of - fixed)
        return jnp.zeros((number_of,), jnp.int32).at[order[jnp.where(places < fixed, places, shifted)]].set(jnp.asarray(lengths, jnp.int32))

    lengths = jnp.where(number % 4 == 0, named(crowded, number // 4), named(common, number - number // 4 - 1))
    mixed = jax.random.permutation(jax.random.fold_in(own, 3), number_of)
    giver, receiver = mixed[0:number_of // 2 * 2:2], mixed[1:number_of // 2 * 2:2]
    slack = jnp.minimum(lengths[giver] - 1, limit - lengths[receiver]) // 2
    slack = jnp.where((giver == order[0]) | (receiver == order[0]) | (lengths[receiver] == 0), 0, jnp.maximum(slack, 0))
    shifted = jax.random.randint(jax.random.fold_in(own, 4), (number_of // 2,), 0, 1 << 20) % (slack + 1)
    lengths = lengths.at[giver].add(-shifted).at[receiver].add(shifted)
    members = jnp.searchsorted(jnp.cumsum(lengths), jnp.arange(rows * top), side="right").astype(jnp.int32)
    table = members.reshape(top, rows).T
    table = table[jax.random.permutation(jax.random.fold_in(own, 1), rows)]
    rotation = jax.random.randint(jax.random.fold_in(own, 2), (rows, 1), 0, top)
    return jnp.take_along_axis(table, (jnp.arange(top)[None, :] + rotation) % top, axis=1)


def shares(count, total, bound, slope, full):
    weights = [(1 << 20) // math.isqrt(grade ** slope) + 1 for grade in range(1, count + 1)]
    largest = bound if full else min(bound, max(-(-total // count), total * weights[0] // sum(weights)))
    least = 1 if total - largest >= count - 1 else 0
    counts, surplus = [largest] + [least] * (count - 1), total - largest - least * (count - 1)
    while surplus > 0:
        candidates = [i for i in range(1, count) if counts[i] < largest] or [i for i in range(1, count) if counts[i] < bound]
        pool, remaining = sum([weights[i] for i in candidates]), surplus
        for i in candidates:
            addition = min(bound - counts[i], max(1, remaining * weights[i] // pool), surplus)
            counts[i] = counts[i] + addition
            surplus = surplus - addition
    return np.array(counts)


def scatter_about(rng, extent, width, limit, shards=(), held_as=jnp.bfloat16):
    values = jax.random.normal(rng, extent, jnp.float32) * width
    if len(shards) > 0:
        values = block_scale(rng, extent, shards, -0.22, 0.18) * values
    return jnp.clip(values, min=-limit, max=limit).astype(held_as)


def setup_inputs(seed: int = 0) -> dict:
    seeds = jax.random.split(jax.random.key(seed), 5)
    spectra = scatter_about(seeds[0], (STATIONS, WINDOWS, 2, F), 1.0, 6.0, ((0, 128), (1, 4)))
    masks = with_ends((jax.random.randint(seeds[1], (STATIONS, WINDOWS), 0, 4) < 3).astype(jnp.int32), jax.random.fold_in(seeds[1], 1), 0, 1)
    pairs = with_ends(jax.random.randint(seeds[2], (PAIRS, 2), 0, STATIONS), jax.random.fold_in(seeds[2], 1), 0, STATIONS - 1).astype(jnp.int32)
    owners_keys = jax.random.split(jax.random.fold_in(seeds[3], 1), PAIRS // PAIR_DEV)
    owners_turns = jax.random.permutation(jax.random.fold_in(seeds[3], 3), PAIRS // PAIR_DEV)
    owners = jax.vmap(lambda own, number: assign_block(jax.random.fold_in(seeds[3], 2), own, number, PAIR_DEV, N_STA, 1, CAP, 2))(owners_keys, owners_turns).reshape((PAIRS, 1))
    return {"spectra": spectra, "masks": masks, "pairs": pairs, "owners": owners}


def lag_table(bins, lags):
    freq = lax.broadcasted_iota(jnp.int32, (bins, lags), 0) + FIRST_BIN
    lag = lax.broadcasted_iota(jnp.int32, (bins, lags), 1) - lags // 2
    turns = freq * lag % SAMPLES
    angle = turns.astype(jnp.float32) * (2.0 * math.pi / SAMPLES)
    scale = bins ** (-0.5)
    return jnp.concatenate([jnp.cos(angle) * scale, -jnp.sin(angle) * scale], 0)

def reference(spectra, masks, pairs, owners):
    spec = spectra.astype(jnp.float32)
    power = lax.optimization_barrier(jnp.mean(spec * spec, axis=(2, 3), keepdims=True))
    whitened = (spec * lax.rsqrt(power + 1e-05)).astype(jnp.bfloat16)
    valid = masks.astype(jnp.float32)
    table = lag_table(F, LAGS)
    blocks = pairs.reshape(N_STA, PAIR_DEV, 2)

    def one_block(block):
        first = whitened[block[:, 0]].astype(jnp.float32)
        second = whitened[block[:, 1]].astype(jnp.float32)
        both = valid[block[:, 0]] * valid[block[:, 1]]
        count = jnp.maximum(lax.optimization_barrier(jnp.sum(both, axis=1)), 1.0)
        real_part = first[:, :, 0] * second[:, :, 0] + first[:, :, 1] * second[:, :, 1]
        imag_part = first[:, :, 1] * second[:, :, 0] - first[:, :, 0] * second[:, :, 1]
        stack = jnp.concatenate([lax.optimization_barrier(jnp.sum(both[:, :, None] * real_part, axis=1)), lax.optimization_barrier(jnp.sum(both[:, :, None] * imag_part, axis=1))], axis=1)
        return jnp.dot(stack, table, precision=lax.Precision.HIGHEST) / count[:, None]
    correlogram = lax.map(one_block, blocks).reshape(PAIRS, LAGS)
    owner = owners[:, 0].reshape(N_STA, PAIR_DEV)
    later = lax.broadcasted_iota(jnp.int32, (PAIR_DEV, PAIR_DEV), 0)
    earlier = lax.broadcasted_iota(jnp.int32, (PAIR_DEV, PAIR_DEV), 1)
    same = (owner[:, :, None] == owner[:, None, :]) & (earlier < later)[None]
    slot = lax.optimization_barrier(jnp.sum(same.astype(jnp.int32), axis=2))
    block_index = lax.broadcasted_iota(jnp.int32, (N_STA, PAIR_DEV), 0)
    target = (owner * SLOTS + block_index * CAP + slot).reshape(PAIRS).astype(jnp.int32)
    stacks = jnp.zeros((OUT_ROWS, LAGS), jnp.float32)
    return stacks.at[target].set(correlogram)
```

```python
import functools
import math

import jax
import jax.numpy as jnp
import ml_dtypes
import numpy as np
from jax import lax
from jax.experimental import pallas as pl
from jax.experimental.pallas import tpu as pltpu
from jax.sharding import PartitionSpec as P

FIRST_BIN = 360
SAMPLES = 180000
MESH = pl.DeviceIdType.MESH
BF = jnp.bfloat16
F32 = jnp.float32
I32 = jnp.int32


def lag_tables(bins, lags):
    freq = np.arange(bins, dtype=np.int64)[:, None] + FIRST_BIN
    lag = np.arange(lags, dtype=np.int64)[None, :] - lags // 2
    angle = (freq * lag % SAMPLES).astype(np.float64) * (2.0 * math.pi / SAMPLES)
    scale = bins ** (-0.5)
    both = np.stack([np.cos(angle) * scale, -np.sin(angle) * scale]).astype(np.float32)
    both = both.reshape(2, 2, 2, bins // 4, lags).transpose(1, 2, 0, 3, 4)
    both = both.reshape(2, 2, bins // 2, lags)
    high = both.astype(ml_dtypes.bfloat16)
    low = (both - high.astype(np.float32)).astype(ml_dtypes.bfloat16)
    return np.stack([high, low], axis=2)


def iota(shape, dim):
    return lax.broadcasted_iota(I32, shape, dim)


def onehot(cond):
    return cond.astype(F32).astype(BF)


def dot(a, b):
    return jnp.dot(a, b, preferred_element_type=F32)


def kernel(
    Y, Z, X,
    spec_ref, list_ref, table_ref, out_ref,
    pka, pkb, p1a, p1b, every_a, every_b, lists, table, r1_out, r1_in, r2_out, r2_in,
    p1a_s, p1a_r, p1b_s, p1b_r, ring_s, ring_r, l2_s, l2_r, l3_s, l3_r, tab_sem,
    r1_s, r1_r, r2_s, r2_r,
):
    D = 2 * Y * Z
    NST = 2 * D
    GA, GB = 2 * Y, 2 * Z
    me = lax.axis_index("sta")
    x = lax.axis_index("win")
    y = me // (2 * Z)
    z = (me // 2) % Z
    c = me % 2
    sib = 1 - c

    def at(yy, zz, cc):
        return (yy * Z + zz) * 2 + cc

    barrier = pltpu.get_barrier_semaphore()

    def greet(sta, win):
        pl.semaphore_signal(barrier, inc=1, device_id=(sta, win), device_id_type=MESH)

    def greet_y(i, carry):
        greet(at((y + i) % Y, z, 0), x)
        greet(at((y + i) % Y, z, 1), x)
        return carry

    def greet_z(i, carry):
        greet(at(y, (z + i) % Z, 0), x)
        greet(at(y, (z + i) % Z, 1), x)
        return carry

    def greet_x(i, carry):
        greet(me, (x + i) % X)
        return carry

    greet(at(y, z, sib), x)
    lax.fori_loop(1, Y, greet_y, 0)
    lax.fori_loop(1, Z, greet_z, 0)
    lax.fori_loop(1, X, greet_x, 0)

    tab_copy = pltpu.make_async_copy(table_ref.at[c], table, tab_sem)
    tab_copy.start()

    bins = spec_ref.shape[3]
    J = bins // 512
    white = []
    for s in range(2):
        v = spec_ref[s, 0].astype(F32)
        power = jnp.sum(jnp.sum(v * v, axis=1, keepdims=True), axis=0, keepdims=True) * (
            1.0 / (2 * bins)
        )
        white.append(v * lax.rsqrt(power + 1e-05))
    for cc in range(2):
        for h, pk in ((0, pka), (1, pkb)):
            rows = []
            for s in range(2):
                for j in range(J):
                    start = (cc * 2 + h) * (bins // 4) + j * 128
                    rows.append(white[s][:, start : start + 128])
            pk[cc, 0 : 4 * J, :] = jnp.concatenate(rows, axis=0).astype(BF)
        pka[cc, 4 * J : 4 * J + 16, :] = list_ref[...]
    PR = 4 * J

    pl.semaphore_wait(barrier, 2 * (Y - 1) + 2 * (Z - 1) + 1 + X - 1)

    slot_a = y * 2 + c
    slot_b = z * 2 + c

    def send_a(yy, cc):
        pltpu.make_async_remote_copy(
            src_ref=pka.at[cc], dst_ref=p1a.at[slot_a], send_sem=p1a_s, recv_sem=p1a_r,
            device_id=(at(yy, z, cc), x), device_id_type=MESH,
        ).start()

    def send_b(zz, cc):
        pltpu.make_async_remote_copy(
            src_ref=pkb.at[cc], dst_ref=p1b.at[slot_b], send_sem=p1b_s, recv_sem=p1b_r,
            device_id=(at(y, zz, cc), x), device_id_type=MESH,
        ).start()

    def loop_a(i, carry):
        send_a((y + i) % Y, 0)
        send_a((y + i) % Y, 1)
        return carry

    def loop_b(i, carry):
        send_b((z + i) % Z, 0)
        send_b((z + i) % Z, 1)
        return carry

    lax.fori_loop(1, Y, loop_a, 0)
    lax.fori_loop(1, Z, loop_b, 0)
    send_a(y, sib)
    send_b(z, sib)
    p1a[slot_a] = pka[c]
    p1b[slot_b] = pkb[c]

    def relayout(group, size):
        n = iota((2 * J * size * 2, size * PR), 0)
        k = iota((2 * J * size * 2, size * PR), 1)
        st = n % (2 * size)
        rij = n // (2 * size)
        ri, j = rij // J, rij % J
        perm = onehot(k == (st // 2) * PR + (st % 2) * 2 * J + j * 2 + ri)
        return dot(perm, group).astype(BF)

    def wait_bytes(ref, sem):
        pltpu.make_async_copy(ref, ref, sem).wait()

    def neighbour(h, step):
        if h == 0:
            return at(y, (z + step + Z) % Z, c)
        return at((y + step + Y) % Y, z, c)

    def ring_copy(h, direction, step, sub):
        every = every_a if h == 0 else every_b
        size, pos = (Z, z) if h == 0 else (Y, y)
        sign = 1 if direction == 0 else -1
        block = (pos - sign * (step - 1) + 2 * size) % size
        half = every.shape[1] // 2
        view = every.at[block, pl.ds(sub * half, half)]
        return pltpu.make_async_remote_copy(
            src_ref=view, dst_ref=view,
            send_sem=ring_s.at[h, direction, step - 1, sub],
            recv_sem=ring_r.at[h, direction, step - 1, sub],
            device_id=(neighbour(h, sign), x), device_id_type=MESH,
        )

    def landed(h, direction, step, sub):
        every = every_a if h == 0 else every_b
        size, pos = (Z, z) if h == 0 else (Y, y)
        sign = 1 if direction == 0 else -1
        block = (pos - sign * step + 2 * size) % size
        half = every.shape[1] // 2
        view = every.at[block, pl.ds(sub * half, half)]
        return pltpu.make_async_remote_copy(
            src_ref=view, dst_ref=view,
            send_sem=ring_s.at[h, direction, step - 1, sub],
            recv_sem=ring_r.at[h, direction, step - 1, sub],
            device_id=(neighbour(h, sign), x), device_id_type=MESH,
        )

    def used(size, direction, step, sub):
        return step < size // 2 or (step == size // 2 and sub == direction)

    def ring_start(h, step):
        size = Z if h == 0 else Y
        for sub in range(2):
            for direction in range(2):
                if used(size, direction, step, sub):
                    if step > 1:
                        landed(h, direction, step - 1, sub).wait_recv()
                    ring_copy(h, direction, step, sub).start()

    def ring_drain(h):
        size = Z if h == 0 else Y
        for direction in range(2):
            for sub in range(2):
                for step in range(1, size // 2 + 1):
                    if used(size, direction, step, sub):
                        forwarded = step < size // 2 and used(size, direction, step + 1, sub)
                        if not forwarded:
                            landed(h, direction, step, sub).wait_recv()

    wait_bytes(p1a.at[pl.ds(0, GA - 1)], p1a_r)
    block = relayout(p1a[:, 0:PR, :].reshape(GA * PR, 128), GA)
    for q in range(2 * J):
        every_a[z, :, q * 128 : (q + 1) * 128] = block[q * 2 * GA : (q + 1) * 2 * GA]
    ring_start(0, 1)

    wait_bytes(p1b.at[pl.ds(0, GB - 1)], p1b_r)
    block = relayout(p1b[...].reshape(GB * PR, 128), GB)
    for q in range(2 * J):
        every_b[y, :, q * 128 : (q + 1) * 128] = block[q * 2 * GB : (q + 1) * 2 * GB]
    ring_start(1, 1)

    share = GA // X
    n = iota((4 * share, GA * 16), 0)
    k = iota((4 * share, GA * 16), 1)
    perm = onehot(k == (x * share + n % share) * 16 + n // share)
    lists[x, z] = dot(perm, p1a[:, PR : PR + 16, :].reshape(GA * 16, 128)).astype(BF)

    def list_z(i, carry):
        pltpu.make_async_remote_copy(
            src_ref=lists.at[x, z], dst_ref=lists.at[x, z], send_sem=l2_s, recv_sem=l2_r,
            device_id=(at(y, (z + i) % Z, c), x), device_id_type=MESH,
        ).start()
        return carry

    def list_x(i, carry):
        pltpu.make_async_remote_copy(
            src_ref=lists.at[x], dst_ref=lists.at[x], send_sem=l3_s, recv_sem=l3_r,
            device_id=(me, (x + i) % X), device_id_type=MESH,
        ).start()
        return carry

    lax.fori_loop(1, Z, list_z, 0)
    if Z // 2 >= 2:
        ring_start(0, 2)
    wait_bytes(lists.at[0, pl.ds(0, Z - 1)], l2_r)
    lax.fori_loop(1, X, list_x, 0)
    if Y // 2 >= 2:
        ring_start(1, 2)
    for step in range(3, max(Y, Z) // 2 + 1):
        if step <= Z // 2:
            ring_start(0, step)
        if step <= Y // 2:
            ring_start(1, step)

    if X > 1:
        wait_bytes(lists.at[pl.ds(0, X - 1)], l3_r)
    n = iota((4 * D, 4 * D), 0)
    k = iota((4 * D, 4 * D), 1)
    d = n % D
    q = n // D
    pos = (d // (2 * Z)) * 2 + d % 2
    src = ((pos // share) * Z + (d // 2) % Z) * (4 * share) + q * share + pos % share
    sorted_lists = dot(onehot(k == src), lists[...].reshape(4 * D, 128))
    first_id = sorted_lists[0:D]
    second_id = sorted_lists[D : 2 * D]
    owner_id = sorted_lists[2 * D : 3 * D]
    mask_rows = sorted_lists[3 * D : 4 * D].astype(BF)
    spread = onehot(iota((NST, D), 0) // 2 == iota((NST, D), 1))
    lane = iota((NST, 128), 1)
    mine = (lane // X == iota((NST, 128), 0) % 2) & (lane < 2 * X)
    fl, fw = iota((128, 128), 0), iota((128, 128), 1)
    fold = onehot((fl < 2 * X) & (fw < X) & (fl % X == fw))
    mask_st = dot(jnp.where(mine, dot(spread, mask_rows), 0.0).astype(BF), fold).astype(BF)
    tri = onehot(iota((128, 128), 0) < iota((128, 128), 1))
    ka = iota((2 * D, NST), 1)
    st_a = ((ka // 4) % Y) * (4 * Z) + (ka // (4 * Y)) * 4 + ka % 4
    st_a = st_a.astype(F32)
    st_b = ka.astype(F32)

    def slots_of(o):
        match = owner_id == o.astype(F32)
        mf = match.astype(F32)
        before = dot(mf.astype(BF), tri)
        picks = [mf * (before == float(i)).astype(F32) for i in range(2)]
        first = jnp.concatenate(
            [jnp.sum(p * (first_id + 1.0), axis=1, keepdims=True) for p in picks], axis=0
        ) - 1.0
        second = jnp.concatenate(
            [jnp.sum(p * (second_id + 1.0), axis=1, keepdims=True) for p in picks], axis=0
        ) - 1.0
        one_b = [onehot(st_b == first), onehot(st_b == second)]
        one_a = [onehot(st_a == first), onehot(st_a == second)]
        both = dot(one_b[0], mask_st) * dot(one_b[1], mask_st)
        count = jnp.maximum(jnp.sum(both, axis=1, keepdims=True), 1.0)
        here = jnp.where(iota(both.shape, 1) == x, both, 0.0)
        return one_a, one_b, jnp.sum(here, axis=1, keepdims=True) / count

    slots = [slots_of(me - c + sib), slots_of(me)]

    ring_drain(0)
    ring_drain(1)
    tab_copy.wait()

    def partial(which):
        one_a, one_b, scale = slots[which]
        quarter = bins // 4
        total = None
        for h, (ones, every) in enumerate(((one_a, every_a), (one_b, every_b))):
            stations = every[...].reshape(NST, 2 * quarter)
            f = dot(ones[0], stations)
            s = dot(ones[1], stations)
            fr, fi = f[:, :quarter], f[:, quarter:]
            sr, si = s[:, :quarter], s[:, quarter:]
            stack = jnp.concatenate([fr * sr + fi * si, fi * sr - fr * si], axis=1)
            high = stack.astype(BF)
            low = (stack - high.astype(F32)).astype(BF)
            part = dot(high, table[h, 0]) + (dot(high, table[h, 1]) + dot(low, table[h, 0]))
            total = part if total is None else total + part
        return total * scale

    r1_out[...] = partial(0)
    r1 = pltpu.make_async_remote_copy(
        src_ref=r1_out, dst_ref=r1_in, send_sem=r1_s, recv_sem=r1_r,
        device_id=(at(y, z, sib), x), device_id_type=MESH,
    )
    r1.start()
    own = partial(1)
    r1.wait_recv()
    own = own + r1_in[...]
    for xx in range(X):
        r2_out[xx] = own[:, xx * 128 : (xx + 1) * 128].astype(BF)
    r1_in[:, 0:128] = own[:, 0:128]
    for xx in range(1, X):
        @pl.when(x == xx)
        def _():
            r1_in[:, 0:128] = own[:, xx * 128 : (xx + 1) * 128]

    def r2_copy(i):
        return pltpu.make_async_remote_copy(
            src_ref=r2_out.at[(x + i) % X], dst_ref=r2_in.at[i], send_sem=r2_s.at[i],
            recv_sem=r2_r.at[i], device_id=(me, (x + i) % X), device_id_type=MESH,
        )

    for i in range(1, X):
        r2_copy(i).start()
    for i in range(1, X):
        r2_copy(i).wait_recv()
    result = r1_in[:, 0:128]
    for i in range(1, X):
        result = result + r2_in[i].astype(F32)
    out_ref[...] = result.reshape(2, D, 128)

    wait_bytes(p1a.at[pl.ds(0, GA - 1)], p1a_s)
    wait_bytes(p1b.at[pl.ds(0, GB - 1)], p1b_s)
    wait_bytes(lists.at[0, pl.ds(0, Z - 1)], l2_s)
    if X > 1:
        wait_bytes(lists.at[pl.ds(0, X - 1)], l3_s)
    for h, size in ((0, Z), (1, Y)):
        for step in range(1, size // 2 + 1):
            for direction in range(2):
                for sub in range(2):
                    if used(size, direction, step, sub):
                        ring_copy(h, direction, step, sub).wait_send()
    r1.wait_send()
    for i in range(1, X):
        r2_copy(i).wait_send()


def body(dims, spectra, masks, pairs, owners):
    Y, Z, X = dims
    bins = spectra.shape[3]
    lags = 128 * X
    D = 2 * Y * Z
    J = bins // 512
    PR = 4 * J
    flat_masks = jnp.pad(masks.reshape(1, 2 * X), ((0, 0), (0, 128 - 2 * X)))
    packet = jnp.concatenate([pairs.T, owners.T, flat_masks], axis=0)
    packet = jnp.pad(packet, ((0, 12), (0, 0))).astype(BF)
    table = jnp.asarray(lag_tables(bins, lags))
    dma = pltpu.SemaphoreType.DMA
    stacks = pl.pallas_call(
        functools.partial(kernel, Y, Z, X),
        out_shape=jax.ShapeDtypeStruct((2, D, 128), F32),
        in_specs=[
            pl.BlockSpec(memory_space=pltpu.VMEM),
            pl.BlockSpec(memory_space=pltpu.VMEM),
            pl.BlockSpec(memory_space=pl.ANY),
        ],
        out_specs=pl.BlockSpec(memory_space=pltpu.VMEM),
        scratch_shapes=[
            pltpu.VMEM((2, PR + 16, 128), BF),
            pltpu.VMEM((2, PR, 128), BF),
            pltpu.VMEM((2 * Y, PR + 16, 128), BF),
            pltpu.VMEM((2 * Z, PR, 128), BF),
            pltpu.VMEM((Z, 4 * Y, 2 * J * 128), BF),
            pltpu.VMEM((Y, 4 * Z, 2 * J * 128), BF),
            pltpu.VMEM((X, Z, 4 * (2 * Y // X), 128), BF),
            pltpu.VMEM((2, 2, bins // 2, lags), BF),
            pltpu.VMEM((2 * D, lags), F32),
            pltpu.VMEM((2 * D, lags), F32),
            pltpu.VMEM((X, 2 * D, 128), BF),
            pltpu.VMEM((X, 2 * D, 128), BF),
            dma, dma, dma, dma,
            dma((2, 2, max(Y, Z) // 2, 2)),
            dma((2, 2, max(Y, Z) // 2, 2)),
            dma, dma, dma, dma, dma,
            dma, dma, dma((X,)), dma((X,)),
        ],
        compiler_params=pltpu.CompilerParams(
            collective_id=0, has_side_effects=True, vmem_limit_bytes=48 * 1024 * 1024
        ),
    )(spectra, packet, table)
    return stacks.transpose(1, 0, 2).reshape(2 * D, 128)


def dims_of(mesh):
    sta, win = mesh.shape["sta"], mesh.shape["win"]
    side = math.isqrt(sta // 2)
    return side, sta // 2 // side, win


def solution(mesh):
    placed = (P("sta", "win", None, None), P("sta", None), P("sta", None), P("sta", None))
    return jax.shard_map(
        functools.partial(body, dims_of(mesh)),
        mesh=mesh, in_specs=placed, out_specs=P("sta", "win"), check_vma=False,
    )
```

```python
import functools
import math

import jax
import jax.numpy as jnp
import ml_dtypes
import numpy as np
from jax import lax
from jax.experimental import pallas as pl
from jax.experimental.pallas import tpu as pltpu
from jax.sharding import PartitionSpec as P

FIRST_BIN = 360
SAMPLES = 180000
WAVES = 2
MESH = pl.DeviceIdType.MESH
BF = jnp.bfloat16
F32 = jnp.float32
I32 = jnp.int32


def lag_tables(bins, lags):
    freq = np.arange(bins, dtype=np.int64)[:, None] + FIRST_BIN
    lag = np.arange(lags, dtype=np.int64)[None, :] - lags // 2
    angle = (freq * lag % SAMPLES).astype(np.float64) * (2.0 * math.pi / SAMPLES)
    scale = bins ** (-0.5)
    both = np.stack([np.cos(angle) * scale, -np.sin(angle) * scale]).astype(np.float32)
    both = both.reshape(2, 2, 2, WAVES, bins // 4 // WAVES, lags // 128, 128)
    both = both.transpose(1, 5, 2, 3, 0, 4, 6)
    both = both.reshape(2, lags // 128, 2, WAVES, bins // 2 // WAVES, 128)
    high = both.astype(ml_dtypes.bfloat16)
    low = (both - high.astype(np.float32)).astype(ml_dtypes.bfloat16)
    return np.stack([high, low], axis=4)


def iota(shape, dim):
    return lax.broadcasted_iota(I32, shape, dim)


def onehot(cond):
    return cond.astype(F32).astype(BF)


def dot(a, b):
    return jnp.dot(a, b, preferred_element_type=F32)


def div(a, n):
    return lax.shift_right_logical(a, jnp.full_like(a, n.bit_length() - 1))


def mod(a, n):
    return a & (n - 1)


def kernel(
    Y, Z, X,
    spec_hbm, mask_hbm, pair_hbm, owner_hbm, table_hbm, out_ref,
    spec_ref, mask_ref, pair_ref, owner_ref, table, perm_a, perm_b, perm_l,
    pka, pkb, p1a, p1b, every_a, every_b, lists, acc, r1_out, r1_in, r2_out, r2_in,
    in_sem, tab_sem, p1a_s, p1a_r, p1b_s, p1b_r, ring_s, ring_r, l2_s, l2_r, l3_s, l3_r,
    r1_s, r1_r, r2_s, r2_r,
):
    D = 2 * Y * Z
    NST = 2 * D
    GA, GB = 2 * Y, 2 * Z
    W = WAVES
    me = lax.axis_index("sta")
    x = lax.axis_index("win")
    y = me // (2 * Z)
    z = (me // 2) % Z
    c = me % 2
    sib = 1 - c

    def at(yy, zz, cc):
        return (yy * Z + zz) * 2 + cc

    inputs = [
        pltpu.make_async_copy(src, dst, in_sem.at[i])
        for i, (src, dst) in enumerate(
            ((spec_hbm, spec_ref), (pair_hbm, pair_ref), (owner_hbm, owner_ref), (mask_hbm, mask_ref))
        )
    ]
    for copy in inputs:
        copy.start()

    barrier = pltpu.get_barrier_semaphore()

    def greet(sta, win):
        pl.semaphore_signal(barrier, inc=1, device_id=(sta, win), device_id_type=MESH)

    def far_first(size):
        return sorted(range(1, size), key=lambda i: -min(i, size - i))

    for i in far_first(Y):
        for cc in range(2):
            greet(at((y + i) % Y, z, cc), x)
    for i in far_first(Z):
        for cc in range(2):
            greet(at(y, (z + i) % Z, cc), x)
    for i in far_first(X):
        greet(me, (x + i) % X)
    greet(at(y, z, sib), x)

    tab_copies = [
        pltpu.make_async_copy(table_hbm.at[c, (x + i) % X], table.at[i], tab_sem.at[i])
        for i in range(X)
    ]
    for copy in tab_copies:
        copy.start()

    bins = spec_ref.shape[3]
    J = bins // 512
    PR = 4 * J
    for copy in inputs:
        copy.wait()
    white = []
    for s in range(2):
        v = spec_ref[s, 0].astype(F32)
        power = jnp.sum(jnp.sum(v * v, axis=1, keepdims=True), axis=0, keepdims=True) * (
            1.0 / (2 * bins)
        )
        white.append(v * lax.rsqrt(power + 1e-05))
    lane = iota((1, 128), 1)
    mask_row = jnp.zeros((1, 128), F32)
    for s in range(2):
        for w in range(X):
            one = mask_ref[s : s + 1, w : w + 1].astype(F32)
            mask_row = jnp.where(lane == s * X + w, one, mask_row)
    packet = jnp.concatenate(
        [
            pair_ref[...].astype(F32), owner_ref[...].astype(F32), mask_row,
            jnp.zeros((12, 128), F32),
        ],
        axis=0,
    ).astype(BF)
    for cc in range(2):
        for h, pk in ((0, pka), (1, pkb)):
            rows = []
            for s in range(2):
                for j in range(J):
                    start = (cc * 2 + h) * (bins // 4) + j * 128
                    rows.append(white[s][:, start : start + 128])
            pk[cc, 0:PR, :] = jnp.concatenate(rows, axis=0).astype(BF)
        pka[cc, PR : PR + 16, :] = packet

    def relayout_perm(size):
        shape = (2 * J * size * 2, size * PR)
        n, k = iota(shape, 0), iota(shape, 1)
        st, rij = mod(n, 2 * size), div(n, 2 * size)
        ri, j = div(rij, J), mod(rij, J)
        return onehot(k == div(st, 2) * PR + mod(st, 2) * 2 * J + j * 2 + ri)

    perm_a[...] = relayout_perm(GA)
    perm_b[...] = relayout_perm(GB)
    share = GA // X
    n, k = iota((4 * share, GA * 16), 0), iota((4 * share, GA * 16), 1)
    perm_l[...] = onehot(k == (x * share + mod(n, share)) * 16 + div(n, share))

    pl.semaphore_wait(barrier, 2 * (Y - 1) + 2 * (Z - 1) + 1 + X - 1)

    slot_a = y * 2 + c
    slot_b = z * 2 + c

    def send_a(yy, cc):
        pltpu.make_async_remote_copy(
            src_ref=pka.at[cc], dst_ref=p1a.at[slot_a], send_sem=p1a_s, recv_sem=p1a_r,
            device_id=(at(yy, z, cc), x), device_id_type=MESH,
        ).start()

    def send_b(zz, cc):
        pltpu.make_async_remote_copy(
            src_ref=pkb.at[cc], dst_ref=p1b.at[slot_b], send_sem=p1b_s, recv_sem=p1b_r,
            device_id=(at(y, zz, cc), x), device_id_type=MESH,
        ).start()

    for i in far_first(Y):
        for cc in range(2):
            send_a((y + i) % Y, cc)
    send_a(y, sib)
    for i in far_first(Z):
        for cc in range(2):
            send_b((z + i) % Z, cc)
    send_b(z, sib)
    p1a[slot_a] = pka[c]
    p1b[slot_b] = pkb[c]

    def wait_bytes(ref, sem):
        pltpu.make_async_copy(ref, ref, sem).wait()

    def hop(h, w, direction, dist):
        every, size, pos = ((every_a, Z, z), (every_b, Y, y))[h]
        sign = 1 - 2 * direction
        parent = 2 if dist > 2 else 0
        to = (pos + sign * (dist - parent) + size) % size
        rows = every.shape[2]

        def view(block):
            if 2 * dist == size:
                return every.at[w, block, pl.ds(direction * (rows // 2), rows // 2)]
            return every.at[w, block]

        sent = view((pos - sign * parent + size) % size)
        comes = view((pos - sign * dist + size) % size)
        sems = (ring_s.at[h, w, direction, dist - 1], ring_r.at[h, w, direction, dist - 1])
        dev = (at(y, to, c) if h == 0 else at(to, z, c), x)
        out, arrive = (
            pltpu.make_async_remote_copy(
                src_ref=v, dst_ref=v, send_sem=sems[0], recv_sem=sems[1],
                device_id=dev, device_id_type=MESH,
            )
            for v in (sent, comes)
        )
        return out, arrive

    half_way = (Z // 2, Y // 2)

    def start_direct(h):
        for w in range(W):
            for dist in range(1, min(2, half_way[h]) + 1):
                for direction in range(2):
                    hop(h, w, direction, dist)[0].start()

    def forward(h, w):
        if half_way[h] > 2:
            for direction in range(2):
                hop(h, w, direction, 2)[1].wait_recv()
                for dist in range(3, half_way[h] + 1):
                    hop(h, w, direction, dist)[0].start()

    def drain(h, w):
        for dist in range(1, half_way[h] + 1):
            if dist == 2 and half_way[h] > 2:
                continue
            for direction in range(2):
                hop(h, w, direction, dist)[1].wait_recv()

    jw = J // W

    def place(every, pos, perm, group, size):
        block = dot(perm[...], group).astype(BF)
        for w in range(W):
            for ri in range(2):
                for j in range(jw):
                    row = (ri * J + w * jw + j) * 2 * size
                    col = (ri * jw + j) * 128
                    every[w, pos, :, col : col + 128] = block[row : row + 2 * size]

    wait_bytes(p1a.at[pl.ds(0, GA - 1)], p1a_r)

    lists[x, z] = dot(perm_l[...], p1a[:, PR : PR + 16, :].reshape(GA * 16, 128)).astype(BF)
    for i in far_first(Z):
        pltpu.make_async_remote_copy(
            src_ref=lists.at[x, z], dst_ref=lists.at[x, z], send_sem=l2_s, recv_sem=l2_r,
            device_id=(at(y, (z + i) % Z, c), x), device_id_type=MESH,
        ).start()

    place(every_a, z, perm_a, p1a[:, 0:PR, :].reshape(GA * PR, 128), GA)
    start_direct(0)
    wait_bytes(p1b.at[pl.ds(0, GB - 1)], p1b_r)
    place(every_b, y, perm_b, p1b[...].reshape(GB * PR, 128), GB)
    start_direct(1)

    forward(0, 0)
    forward(1, 0)
    if Z > 1:
        wait_bytes(lists.at[0, pl.ds(0, Z - 1)], l2_r)
    for i in far_first(X):
        pltpu.make_async_remote_copy(
            src_ref=lists.at[x], dst_ref=lists.at[x], send_sem=l3_s, recv_sem=l3_r,
            device_id=(me, (x + i) % X), device_id_type=MESH,
        ).start()
    for w in range(1, W):
        forward(0, w)
        forward(1, w)

    n, k = iota((4 * D, 4 * D), 0), iota((4 * D, 4 * D), 1)
    d, q = mod(n, D), div(n, D)
    pos = div(d, 2 * Z) * 2 + mod(d, 2)
    src = (div(pos, share) * Z + mod(div(d, 2), Z)) * (4 * share) + q * share + mod(pos, share)
    perm = onehot(k == src)
    if X > 1:
        wait_bytes(lists.at[pl.ds(0, X - 1)], l3_r)
    sorted_lists = dot(perm, lists[...].reshape(4 * D, 128))
    first_id = sorted_lists[0:D]
    second_id = sorted_lists[D : 2 * D]
    owner_id = sorted_lists[2 * D : 3 * D]
    mask_rows = sorted_lists[3 * D : 4 * D].astype(BF)
    spread = onehot(div(iota((NST, D), 0), 2) == iota((NST, D), 1))
    lane = iota((NST, 128), 1)
    mine = (div(lane, X) == mod(iota((NST, 128), 0), 2)) & (lane < 2 * X)
    fl, fw = iota((128, 128), 0), iota((128, 128), 1)
    fold = onehot((fl < 2 * X) & (fw < X) & (mod(fl, X) == fw))
    mask_st = dot(jnp.where(mine, dot(spread, mask_rows), 0.0).astype(BF), fold).astype(BF)
    tri = onehot(iota((128, 128), 0) < iota((128, 128), 1))
    ka = iota((2 * D, NST), 1)
    st_a = mod(div(ka, 4), Y) * (4 * Z) + div(ka, 4 * Y) * 4 + mod(ka, 4)
    st_a = st_a.astype(F32)
    st_b = ka.astype(F32)

    def slots_of(o):
        match = owner_id == o.astype(F32)
        mf = match.astype(F32)
        before = dot(mf.astype(BF), tri)
        picks = [mf * (before == float(i)).astype(F32) for i in range(2)]
        first = jnp.concatenate(
            [jnp.sum(p * (first_id + 1.0), axis=1, keepdims=True) for p in picks], axis=0
        ) - 1.0
        second = jnp.concatenate(
            [jnp.sum(p * (second_id + 1.0), axis=1, keepdims=True) for p in picks], axis=0
        ) - 1.0
        one_b = [onehot(st_b == first), onehot(st_b == second)]
        one_a = [onehot(st_a == first), onehot(st_a == second)]
        both = dot(one_b[0], mask_st) * dot(one_b[1], mask_st)
        count = jnp.maximum(jnp.sum(both, axis=1, keepdims=True), 1.0)
        here = jnp.where(iota(both.shape, 1) == x, both, 0.0)
        return (one_a, one_b), jnp.sum(here, axis=1, keepdims=True) / count

    slots = [slots_of(me - c + sib), slots_of(me)]
    for copy in tab_copies:
        copy.wait()

    if X == 4:
        sides = ((2, 1), (3, 0))
    elif X == 2:
        sides = ((1,), (0,))
    else:
        sides = ((0,),)
    quarter = bins // 4 // W

    def stack_of(which, w):
        parts = []
        for h, every in enumerate((every_a, every_b)):
            ones = slots[which][0][h]
            stations = every[w].reshape(NST, 2 * quarter)
            f = dot(ones[0], stations)
            s = dot(ones[1], stations)
            fr, fi = f[:, :quarter], f[:, quarter:]
            sr, si = s[:, :quarter], s[:, quarter:]
            stack = jnp.concatenate([fr * sr + fi * si, fi * sr - fr * si], axis=1)
            high = stack.astype(BF)
            low = (stack - high.astype(F32)).astype(BF)
            parts.append((high, low))
        return parts

    def product(parts, w, side):
        total = None
        for h, (high, low) in enumerate(parts):
            t_high, t_low = (
                jnp.concatenate([table[i, h, w, p] for i in sides[side]], axis=1)
                for p in range(2)
            )
            part = dot(high, t_high) + (dot(high, t_low) + dot(low, t_high))
            total = part if total is None else total + part
        return total

    NS = len(sides)
    wide = 128 * len(sides[0])
    for w in range(W - 1):
        drain(0, w)
        drain(1, w)
        for which in range(2):
            parts = stack_of(which, w)
            for side in range(NS):
                value = product(parts, w, side)
                if w > 0:
                    value = value + acc[which, side]
                acc[which, side] = value
    w = W - 1
    drain(0, w)
    drain(1, w)

    def finish(which, side, parts):
        value = product(parts, w, side)
        if W > 1:
            value = value + acc[which, side]
        return value * slots[which][1]

    def r1_copy(side):
        return pltpu.make_async_remote_copy(
            src_ref=r1_out.at[side], dst_ref=r1_in.at[side], send_sem=r1_s.at[side],
            recv_sem=r1_r.at[side], device_id=(at(y, z, sib), x), device_id_type=MESH,
        )

    def r2_copy(i):
        return pltpu.make_async_remote_copy(
            src_ref=r2_out.at[i], dst_ref=r2_in.at[i], send_sem=r2_s.at[i],
            recv_sem=r2_r.at[i], device_id=(me, (x + i) % X), device_id_type=MESH,
        )

    parts = stack_of(0, w)
    for side in range(NS):
        r1_out[side] = finish(0, side, parts)
        r1_copy(side).start()
    parts = stack_of(1, w)
    for side in range(NS):
        acc[1, side] = finish(1, side, parts)
    for side in range(NS):
        r1_copy(side).wait_recv()
        for m, i in enumerate(sides[side]):
            piece = acc[1, side, :, m * 128 : (m + 1) * 128] + r1_in[side, :, m * 128 : (m + 1) * 128]
            if i > 0:
                r2_out[i] = piece.astype(BF)
                r2_copy(i).start()
            else:
                result = piece
    for i in range(1, X):
        r2_copy(i).wait_recv()
        result = result + r2_in[i].astype(F32)
    out_ref[...] = result.reshape(2, D, 128)

    wait_bytes(p1a.at[pl.ds(0, GA - 1)], p1a_s)
    wait_bytes(p1b.at[pl.ds(0, GB - 1)], p1b_s)
    if Z > 1:
        wait_bytes(lists.at[0, pl.ds(0, Z - 1)], l2_s)
    if X > 1:
        wait_bytes(lists.at[pl.ds(0, X - 1)], l3_s)
    for h in range(2):
        for w in range(W):
            for direction in range(2):
                for dist in range(1, half_way[h] + 1):
                    hop(h, w, direction, dist)[0].wait_send()
    for side in range(NS):
        r1_copy(side).wait_send()
    for i in range(1, X):
        r2_copy(i).wait_send()


def body(dims, spectra, masks, pairs, owners):
    Y, Z, X = dims
    bins = spectra.shape[3]
    lags = 128 * X
    D = 2 * Y * Z
    J = bins // 512
    PR = 4 * J
    W = WAVES
    table = jnp.asarray(lag_tables(bins, lags))
    sides = 2 if X > 1 else 1
    wide = lags // sides
    dma = pltpu.SemaphoreType.DMA
    stacks = pl.pallas_call(
        functools.partial(kernel, Y, Z, X),
        out_shape=jax.ShapeDtypeStruct((2, D, 128), F32),
        in_specs=[pl.BlockSpec(memory_space=pl.ANY)] * 5,
        out_specs=pl.BlockSpec(memory_space=pltpu.VMEM),
        scratch_shapes=[
            pltpu.VMEM(spectra.shape, BF),
            pltpu.VMEM(masks.shape, I32),
            pltpu.VMEM((2, 128), I32),
            pltpu.VMEM((1, 128), I32),
            pltpu.VMEM(table.shape[1:], BF),
            pltpu.VMEM((8 * J * Y, 2 * Y * PR), BF),
            pltpu.VMEM((8 * J * Z, 2 * Z * PR), BF),
            pltpu.VMEM((4 * (2 * Y // X), 2 * Y * 16), BF),
            pltpu.VMEM((2, PR + 16, 128), BF),
            pltpu.VMEM((2, PR, 128), BF),
            pltpu.VMEM((2 * Y, PR + 16, 128), BF),
            pltpu.VMEM((2 * Z, PR, 128), BF),
            pltpu.VMEM((W, Z, 4 * Y, 2 * J * 128 // W), BF),
            pltpu.VMEM((W, Y, 4 * Z, 2 * J * 128 // W), BF),
            pltpu.VMEM((X, Z, 4 * (2 * Y // X), 128), BF),
            pltpu.VMEM((2, sides, 2 * D, wide), F32),
            pltpu.VMEM((sides, 2 * D, wide), F32),
            pltpu.VMEM((sides, 2 * D, wide), F32),
            pltpu.VMEM((X, 2 * D, 128), BF),
            pltpu.VMEM((X, 2 * D, 128), BF),
            dma((4,)), dma((X,)), dma, dma, dma, dma,
            dma((2, W, 2, max(Y, Z) // 2)),
            dma((2, W, 2, max(Y, Z) // 2)),
            dma, dma, dma, dma,
            dma((sides,)), dma((sides,)), dma((X,)), dma((X,)),
        ],
        compiler_params=pltpu.CompilerParams(
            collective_id=0, has_side_effects=True, vmem_limit_bytes=48 * 1024 * 1024
        ),
    )(spectra, masks, pairs.T, owners.T, table)
    return stacks.transpose(1, 0, 2).reshape(2 * D, 128)


def dims_of(mesh):
    sta, win = mesh.shape["sta"], mesh.shape["win"]
    side = math.isqrt(sta // 2)
    return side, sta // 2 // side, win


def solution(mesh):
    placed = (P("sta", "win", None, None), P("sta", None), P("sta", None), P("sta", None))
    return jax.shard_map(
        functools.partial(body, dims_of(mesh)),
        mesh=mesh, in_specs=placed, out_specs=P("sta", "win"), check_vma=False,
    )
```

```python
import functools
import math

import jax
import jax.numpy as jnp
import ml_dtypes
import numpy as np
from jax import lax
from jax.experimental import pallas as pl
from jax.experimental.pallas import tpu as pltpu
from jax.sharding import PartitionSpec as P

FIRST_BIN = 360
SAMPLES = 180000
WAVES = 2
MESH = pl.DeviceIdType.MESH
BF = jnp.bfloat16
F32 = jnp.float32
I32 = jnp.int32


def lag_tables(bins, lags):
    freq = np.arange(bins, dtype=np.int64)[:, None] + FIRST_BIN
    lag = np.arange(lags, dtype=np.int64)[None, :] - lags // 2
    angle = (freq * lag % SAMPLES).astype(np.float64) * (2.0 * math.pi / SAMPLES)
    scale = bins ** (-0.5)
    both = np.stack([np.cos(angle) * scale, -np.sin(angle) * scale]).astype(np.float32)
    both = both.reshape(2, 2, 2, WAVES, bins // 4 // WAVES, lags // 128, 128)
    both = both.transpose(1, 5, 2, 3, 0, 4, 6)
    both = both.reshape(2, lags // 128, 2, WAVES, bins // 2 // WAVES, 128)
    high = both.astype(ml_dtypes.bfloat16)
    low = (both - high.astype(np.float32)).astype(ml_dtypes.bfloat16)
    return np.stack([high, low], axis=4)


def iota(shape, dim):
    return lax.broadcasted_iota(I32, shape, dim)


def onehot(cond):
    return cond.astype(F32).astype(BF)


def dot(a, b):
    return jnp.dot(a, b, preferred_element_type=F32)


def div(a, n):
    return lax.shift_right_logical(a, jnp.full_like(a, n.bit_length() - 1))


def mod(a, n):
    return a & (n - 1)


def kernel(
    Y, Z, X,
    spec_hbm, mask_hbm, pair_hbm, owner_hbm, table_hbm, out_ref,
    spec_ref, mask_ref, pair_ref, owner_ref, table, perm_a, perm_b, perm_l, perm_s,
    pka, pkb, p1a, p1b, every_a, every_b, lists, acc, r1_out, r1_in, r2_out, r2_in,
    in_sem, tab_sem, p1a_s, p1a_r, p1b_s, p1b_r, ring_s, ring_r, l2_s, l2_r, l3_s, l3_r,
    r1_s, r1_r, r2_s, r2_r,
):
    D = 2 * Y * Z
    NST = 2 * D
    GA, GB = 2 * Y, 2 * Z
    W = WAVES
    me = lax.axis_index("sta")
    x = lax.axis_index("win")
    y = me // (2 * Z)
    z = (me // 2) % Z
    c = me % 2
    sib = 1 - c

    def at(yy, zz, cc):
        return (yy * Z + zz) * 2 + cc

    inputs = [
        pltpu.make_async_copy(src, dst, in_sem.at[i])
        for i, (src, dst) in enumerate(
            ((spec_hbm, spec_ref), (pair_hbm, pair_ref), (owner_hbm, owner_ref), (mask_hbm, mask_ref))
        )
    ]
    for copy in inputs:
        copy.start()

    barrier = pltpu.get_barrier_semaphore()

    def greet(sta, win):
        pl.semaphore_signal(barrier, inc=1, device_id=(sta, win), device_id_type=MESH)

    def far_first(size):
        return sorted(range(1, size), key=lambda i: -min(i, size - i))

    for i in far_first(Y):
        for cc in range(2):
            greet(at((y + i) % Y, z, cc), x)
    for i in far_first(Z):
        for cc in range(2):
            greet(at(y, (z + i) % Z, cc), x)
    for i in far_first(X):
        greet(me, (x + i) % X)
    greet(at(y, z, sib), x)

    bins = spec_ref.shape[3]
    J = bins // 512
    PR = 4 * J
    for copy in inputs:
        copy.wait()
    white = []
    for s in range(2):
        v = spec_ref[s, 0].astype(F32)
        power = jnp.sum(jnp.sum(v * v, axis=1, keepdims=True), axis=0, keepdims=True) * (
            1.0 / (2 * bins)
        )
        white.append(v * lax.rsqrt(power + 1e-05))
    lane = iota((1, 128), 1)
    mask_row = jnp.zeros((1, 128), F32)
    for s in range(2):
        for w in range(X):
            one = mask_ref[s : s + 1, w : w + 1].astype(F32)
            mask_row = jnp.where(lane == s * X + w, one, mask_row)
    packet = jnp.concatenate(
        [
            pair_ref[...].astype(F32), owner_ref[...].astype(F32), mask_row,
            jnp.zeros((12, 128), F32),
        ],
        axis=0,
    ).astype(BF)
    for cc in range(2):
        for h, pk in ((0, pka), (1, pkb)):
            rows = []
            for s in range(2):
                for j in range(J):
                    start = (cc * 2 + h) * (bins // 4) + j * 128
                    rows.append(white[s][:, start : start + 128])
            pk[cc, 0:PR, :] = jnp.concatenate(rows, axis=0).astype(BF)
        pka[cc, PR : PR + 16, :] = packet

    def relayout_perm(size):
        shape = (2 * J * size * 2, size * PR)
        n, k = iota(shape, 0), iota(shape, 1)
        st, rij = mod(n, 2 * size), div(n, 2 * size)
        ri, j = div(rij, J), mod(rij, J)
        return onehot(k == div(st, 2) * PR + mod(st, 2) * 2 * J + j * 2 + ri)

    pl.semaphore_wait(barrier, 2 * (Y - 1) + 2 * (Z - 1) + 1 + X - 1)

    slot_a = y * 2 + c
    slot_b = z * 2 + c

    def send_a(yy, cc):
        pltpu.make_async_remote_copy(
            src_ref=pka.at[cc], dst_ref=p1a.at[slot_a], send_sem=p1a_s, recv_sem=p1a_r,
            device_id=(at(yy, z, cc), x), device_id_type=MESH,
        ).start()

    def send_b(zz, cc):
        pltpu.make_async_remote_copy(
            src_ref=pkb.at[cc], dst_ref=p1b.at[slot_b], send_sem=p1b_s, recv_sem=p1b_r,
            device_id=(at(y, zz, cc), x), device_id_type=MESH,
        ).start()

    for i in far_first(Y):
        for cc in range(2):
            send_a((y + i) % Y, cc)
    send_a(y, sib)
    for i in far_first(Z):
        for cc in range(2):
            send_b((z + i) % Z, cc)
    send_b(z, sib)
    p1a[slot_a] = pka[c]
    p1b[slot_b] = pkb[c]

    tab_copies = [
        pltpu.make_async_copy(table_hbm.at[c, (x + i) % X], table.at[i], tab_sem.at[i])
        for i in range(X)
    ]
    for copy in tab_copies:
        copy.start()

    perm_a[...] = relayout_perm(GA)
    perm_b[...] = relayout_perm(GB)
    share = GA // X
    n, k = iota((4 * share, GA * 16), 0), iota((4 * share, GA * 16), 1)
    perm_l[...] = onehot(k == (x * share + mod(n, share)) * 16 + div(n, share))

    def wait_bytes(ref, sem):
        pltpu.make_async_copy(ref, ref, sem).wait()

    def hop(h, w, direction, dist):
        every, size, pos = ((every_a, Z, z), (every_b, Y, y))[h]
        sign = 1 - 2 * direction
        parent = 2 if dist > 2 else 0
        to = (pos + sign * (dist - parent) + size) % size
        rows = every.shape[2]

        def view(block):
            if 2 * dist == size:
                return every.at[w, block, pl.ds(direction * (rows // 2), rows // 2)]
            return every.at[w, block]

        sent = view((pos - sign * parent + size) % size)
        comes = view((pos - sign * dist + size) % size)
        sems = (ring_s.at[h, w, direction, dist - 1], ring_r.at[h, w, direction, dist - 1])
        dev = (at(y, to, c) if h == 0 else at(to, z, c), x)
        out, arrive = (
            pltpu.make_async_remote_copy(
                src_ref=v, dst_ref=v, send_sem=sems[0], recv_sem=sems[1],
                device_id=dev, device_id_type=MESH,
            )
            for v in (sent, comes)
        )
        return out, arrive

    half_way = (Z // 2, Y // 2)

    def start_direct(h):
        for w in range(W):
            for dist in (2, 1):
                if dist <= half_way[h]:
                    for direction in range(2):
                        hop(h, w, direction, dist)[0].start()

    def forward(h, w):
        if half_way[h] > 2:
            for direction in range(2):
                hop(h, w, direction, 2)[1].wait_recv()
                for dist in range(3, half_way[h] + 1):
                    hop(h, w, direction, dist)[0].start()

    def drain(h, w):
        for dist in range(1, half_way[h] + 1):
            if dist == 2 and half_way[h] > 2:
                continue
            for direction in range(2):
                hop(h, w, direction, dist)[1].wait_recv()

    jw = J // W

    def place(every, pos, perm, group, size):
        block = dot(perm[...], group).astype(BF)
        for w in range(W):
            for ri in range(2):
                for j in range(jw):
                    row = (ri * J + w * jw + j) * 2 * size
                    col = (ri * jw + j) * 128
                    every[w, pos, :, col : col + 128] = block[row : row + 2 * size]

    wait_bytes(p1a.at[pl.ds(0, GA - 1)], p1a_r)

    def lists_x():
        if Z > 1:
            wait_bytes(lists.at[0, pl.ds(0, Z - 1)], l2_r)
        for i in far_first(X):
            pltpu.make_async_remote_copy(
                src_ref=lists.at[x], dst_ref=lists.at[x], send_sem=l3_s, recv_sem=l3_r,
                device_id=(me, (x + i) % X), device_id_type=MESH,
            ).start()

    def prepare():
        n, k = iota((4 * D, 4 * D), 0), iota((4 * D, 4 * D), 1)
        d, q = mod(n, D), div(n, D)
        pos = div(d, 2 * Z) * 2 + mod(d, 2)
        src = (div(pos, share) * Z + mod(div(d, 2), Z)) * (4 * share) + q * share + mod(pos, share)
        perm_s[...] = onehot(k == src)

    def lists_z():
        lists[x, z] = dot(perm_l[...], p1a[:, PR : PR + 16, :].reshape(GA * 16, 128)).astype(BF)
        for i in far_first(Z):
            pltpu.make_async_remote_copy(
                src_ref=lists.at[x, z], dst_ref=lists.at[x, z], send_sem=l2_s, recv_sem=l2_r,
                device_id=(at(y, (z + i) % Z, c), x), device_id_type=MESH,
            ).start()

    lists_z()

    place(every_a, z, perm_a, p1a[:, 0:PR, :].reshape(GA * PR, 128), GA)
    start_direct(0)
    wait_bytes(p1b.at[pl.ds(0, GB - 1)], p1b_r)
    place(every_b, y, perm_b, p1b[...].reshape(GB * PR, 128), GB)
    start_direct(1)
    prepare()
    lists_x()

    forward(0, 0)
    forward(1, 0)
    for w in range(1, W):
        forward(0, w)
        forward(1, w)

    if X > 1:
        wait_bytes(lists.at[pl.ds(0, X - 1)], l3_r)
    sorted_lists = dot(perm_s[...], lists[...].reshape(4 * D, 128))
    first_id = sorted_lists[0:D]
    second_id = sorted_lists[D : 2 * D]
    owner_id = sorted_lists[2 * D : 3 * D]
    mask_rows = sorted_lists[3 * D : 4 * D].astype(BF)
    spread = onehot(div(iota((NST, D), 0), 2) == iota((NST, D), 1))
    lane = iota((NST, 128), 1)
    mine = (div(lane, X) == mod(iota((NST, 128), 0), 2)) & (lane < 2 * X)
    fl, fw = iota((128, 128), 0), iota((128, 128), 1)
    fold = onehot((fl < 2 * X) & (fw < X) & (mod(fl, X) == fw))
    mask_st = dot(jnp.where(mine, dot(spread, mask_rows), 0.0).astype(BF), fold).astype(BF)
    tri = onehot(iota((128, 128), 0) < iota((128, 128), 1))
    ka = iota((2 * D, NST), 1)
    st_a = mod(div(ka, 4), Y) * (4 * Z) + div(ka, 4 * Y) * 4 + mod(ka, 4)
    st_a = st_a.astype(F32)
    st_b = ka.astype(F32)

    def slots_of(o):
        match = owner_id == o.astype(F32)
        mf = match.astype(F32)
        before = dot(mf.astype(BF), tri)
        picks = [mf * (before == float(i)).astype(F32) for i in range(2)]
        first = jnp.concatenate(
            [jnp.sum(p * (first_id + 1.0), axis=1, keepdims=True) for p in picks], axis=0
        ) - 1.0
        second = jnp.concatenate(
            [jnp.sum(p * (second_id + 1.0), axis=1, keepdims=True) for p in picks], axis=0
        ) - 1.0
        one_b = [onehot(st_b == first), onehot(st_b == second)]
        one_a = [onehot(st_a == first), onehot(st_a == second)]
        both = dot(one_b[0], mask_st) * dot(one_b[1], mask_st)
        count = jnp.maximum(jnp.sum(both, axis=1, keepdims=True), 1.0)
        here = jnp.where(iota(both.shape, 1) == x, both, 0.0)
        return (one_a, one_b), jnp.sum(here, axis=1, keepdims=True) / count

    slots = [slots_of(me - c + sib), slots_of(me)]
    for copy in tab_copies:
        copy.wait()

    if X == 4:
        sides = ((2, 1), (3, 0))
    elif X == 2:
        sides = ((1,), (0,))
    else:
        sides = ((0,),)
    quarter = bins // 4 // W

    def stack_of(which, w):
        parts = []
        for h, every in enumerate((every_a, every_b)):
            ones = slots[which][0][h]
            stations = every[w].reshape(NST, 2 * quarter)
            f = dot(ones[0], stations)
            s = dot(ones[1], stations)
            fr, fi = f[:, :quarter], f[:, quarter:]
            sr, si = s[:, :quarter], s[:, quarter:]
            stack = jnp.concatenate([fr * sr + fi * si, fi * sr - fr * si], axis=1)
            high = stack.astype(BF)
            low = (stack - high.astype(F32)).astype(BF)
            parts.append((high, low))
        return parts

    def product(parts, w, side):
        total = None
        for h, (high, low) in enumerate(parts):
            t_high, t_low = (
                jnp.concatenate([table[i, h, w, p] for i in sides[side]], axis=1)
                for p in range(2)
            )
            part = dot(high, t_high) + (dot(high, t_low) + dot(low, t_high))
            total = part if total is None else total + part
        return total

    NS = len(sides)
    wide = 128 * len(sides[0])
    for w in range(W - 1):
        drain(0, w)
        drain(1, w)
        for which in range(2):
            parts = stack_of(which, w)
            for side in range(NS):
                value = product(parts, w, side)
                if w > 0:
                    value = value + acc[which, side]
                acc[which, side] = value
    w = W - 1
    drain(0, w)
    drain(1, w)

    def finish(which, side, parts):
        value = product(parts, w, side)
        if W > 1:
            value = value + acc[which, side]
        return value * slots[which][1]

    def r1_copy(side):
        return pltpu.make_async_remote_copy(
            src_ref=r1_out.at[side], dst_ref=r1_in.at[side], send_sem=r1_s.at[side],
            recv_sem=r1_r.at[side], device_id=(at(y, z, sib), x), device_id_type=MESH,
        )

    def r2_copy(i):
        return pltpu.make_async_remote_copy(
            src_ref=r2_out.at[i], dst_ref=r2_in.at[i], send_sem=r2_s.at[i],
            recv_sem=r2_r.at[i], device_id=(me, (x + i) % X), device_id_type=MESH,
        )

    parts = stack_of(0, w)
    for side in range(NS):
        r1_out[side] = finish(0, side, parts)
        r1_copy(side).start()
    parts = stack_of(1, w)
    for side in range(NS):
        acc[1, side] = finish(1, side, parts)
    for side in range(NS):
        r1_copy(side).wait_recv()
        for m, i in enumerate(sides[side]):
            piece = acc[1, side, :, m * 128 : (m + 1) * 128] + r1_in[side, :, m * 128 : (m + 1) * 128]
            if i > 0:
                r2_out[i] = piece.astype(BF)
                r2_copy(i).start()
            else:
                result = piece
    for i in range(1, X):
        r2_copy(i).wait_recv()
        result = result + r2_in[i].astype(F32)
    out_ref[...] = result.reshape(2, D, 128)

    wait_bytes(p1a.at[pl.ds(0, GA - 1)], p1a_s)
    wait_bytes(p1b.at[pl.ds(0, GB - 1)], p1b_s)
    if Z > 1:
        wait_bytes(lists.at[0, pl.ds(0, Z - 1)], l2_s)
    if X > 1:
        wait_bytes(lists.at[pl.ds(0, X - 1)], l3_s)
    for h in range(2):
        for w in range(W):
            for direction in range(2):
                for dist in range(1, half_way[h] + 1):
                    hop(h, w, direction, dist)[0].wait_send()
    for side in range(NS):
        r1_copy(side).wait_send()
    for i in range(1, X):
        r2_copy(i).wait_send()


def body(dims, spectra, masks, pairs, owners):
    Y, Z, X = dims
    bins = spectra.shape[3]
    lags = 128 * X
    D = 2 * Y * Z
    J = bins // 512
    PR = 4 * J
    W = WAVES
    table = jnp.asarray(lag_tables(bins, lags))
    sides = 2 if X > 1 else 1
    wide = lags // sides
    dma = pltpu.SemaphoreType.DMA
    stacks = pl.pallas_call(
        functools.partial(kernel, Y, Z, X),
        out_shape=jax.ShapeDtypeStruct((2, D, 128), F32),
        in_specs=[pl.BlockSpec(memory_space=pl.ANY)] * 5,
        out_specs=pl.BlockSpec(memory_space=pltpu.VMEM),
        scratch_shapes=[
            pltpu.VMEM(spectra.shape, BF),
            pltpu.VMEM(masks.shape, I32),
            pltpu.VMEM((2, 128), I32),
            pltpu.VMEM((1, 128), I32),
            pltpu.VMEM(table.shape[1:], BF),
            pltpu.VMEM((8 * J * Y, 2 * Y * PR), BF),
            pltpu.VMEM((8 * J * Z, 2 * Z * PR), BF),
            pltpu.VMEM((4 * (2 * Y // X), 2 * Y * 16), BF),
            pltpu.VMEM((4 * D, 4 * D), BF),
            pltpu.VMEM((2, PR + 16, 128), BF),
            pltpu.VMEM((2, PR, 128), BF),
            pltpu.VMEM((2 * Y, PR + 16, 128), BF),
            pltpu.VMEM((2 * Z, PR, 128), BF),
            pltpu.VMEM((W, Z, 4 * Y, 2 * J * 128 // W), BF),
            pltpu.VMEM((W, Y, 4 * Z, 2 * J * 128 // W), BF),
            pltpu.VMEM((X, Z, 4 * (2 * Y // X), 128), BF),
            pltpu.VMEM((2, sides, 2 * D, wide), F32),
            pltpu.VMEM((sides, 2 * D, wide), F32),
            pltpu.VMEM((sides, 2 * D, wide), F32),
            pltpu.VMEM((X, 2 * D, 128), BF),
            pltpu.VMEM((X, 2 * D, 128), BF),
            dma((4,)), dma((X,)), dma, dma, dma, dma,
            dma((2, W, 2, max(Y, Z) // 2)),
            dma((2, W, 2, max(Y, Z) // 2)),
            dma, dma, dma, dma,
            dma((sides,)), dma((sides,)), dma((X,)), dma((X,)),
        ],
        compiler_params=pltpu.CompilerParams(
            collective_id=0, has_side_effects=True, vmem_limit_bytes=63 * 1024 * 1024
        ),
    )(spectra, masks, pairs.T, owners.T, table)
    return stacks.transpose(1, 0, 2).reshape(2 * D, 128)


def dims_of(mesh):
    sta, win = mesh.shape["sta"], mesh.shape["win"]
    side = math.isqrt(sta // 2)
    return side, sta // 2 // side, win


def solution(mesh):
    placed = (P("sta", "win", None, None), P("sta", None), P("sta", None), P("sta", None))
    return jax.shard_map(
        functools.partial(body, dims_of(mesh)),
        mesh=mesh, in_specs=placed, out_specs=P("sta", "win"), check_vma=False,
    )
```

```python
import functools
import math

import jax
import jax.numpy as jnp
import ml_dtypes
import numpy as np
from jax import lax
from jax.experimental import pallas as pl
from jax.experimental.pallas import tpu as pltpu
from jax.sharding import PartitionSpec as P

FIRST_BIN = 360
SAMPLES = 180000
WAVES = 2
MESH = pl.DeviceIdType.MESH
BF = jnp.bfloat16
F32 = jnp.float32
I32 = jnp.int32


def lag_tables(bins, lags):
    freq = np.arange(bins, dtype=np.int64)[:, None] + FIRST_BIN
    lag = np.arange(lags, dtype=np.int64)[None, :] - lags // 2
    angle = (freq * lag % SAMPLES).astype(np.float64) * (2.0 * math.pi / SAMPLES)
    scale = bins ** (-0.5)
    both = np.stack([np.cos(angle) * scale, -np.sin(angle) * scale]).astype(np.float32)
    both = both.reshape(2, 2, 2, WAVES, bins // 4 // WAVES, lags // 128, 128)
    both = both.transpose(1, 5, 2, 3, 0, 4, 6)
    both = both.reshape(2, lags // 128, 2, WAVES, bins // 2 // WAVES, 128)
    high = both.astype(ml_dtypes.bfloat16)
    low = (both - high.astype(np.float32)).astype(ml_dtypes.bfloat16)
    return np.stack([high, low], axis=4)


def iota(shape, dim):
    return lax.broadcasted_iota(I32, shape, dim)


def onehot(cond):
    return cond.astype(F32).astype(BF)


def dot(a, b):
    return jnp.dot(a, b, preferred_element_type=F32)


def div(a, n):
    return lax.shift_right_logical(a, jnp.full_like(a, n.bit_length() - 1))


def mod(a, n):
    return a & (n - 1)


def kernel(
    Y, Z, X,
    spec_hbm, mask_hbm, pair_hbm, owner_hbm, table_hbm, own_hbm, r2_in,
    spec_ref, mask_ref, pair_ref, owner_ref, table, perm_a, perm_b, perm_l, perm_s,
    pka, pkb, p1a, p1b, every_a, every_b, lists, acc, r1_out, r1_in, r2_out, own, ids,
    in_sem, tab_sem, p1a_s, p1a_r, p1b_s, p1b_r, ring_s, ring_r, l2_s, l2_r, l3_s, l3_r,
    r1_s, r1_r, r2_s, r2_r, own_s,
):
    D = 2 * Y * Z
    NST = 2 * D
    GA, GB = 2 * Y, 2 * Z
    W = WAVES
    me = lax.axis_index("sta")
    x = lax.axis_index("win")
    y = me // (2 * Z)
    z = (me // 2) % Z
    c = me % 2
    sib = 1 - c

    def at(yy, zz, cc):
        return (yy * Z + zz) * 2 + cc

    inputs = [
        pltpu.make_async_copy(src, dst, in_sem.at[i])
        for i, (src, dst) in enumerate(
            ((spec_hbm, spec_ref), (pair_hbm, pair_ref), (owner_hbm, owner_ref), (mask_hbm, mask_ref))
        )
    ]
    for copy in inputs:
        copy.start()

    barrier = pltpu.get_barrier_semaphore()

    def greet(sta, win):
        pl.semaphore_signal(barrier, inc=1, device_id=(sta, win), device_id_type=MESH)

    def far_first(size):
        return sorted(range(1, size), key=lambda i: -min(i, size - i))

    for i in far_first(Y):
        for cc in range(2):
            greet(at((y + i) % Y, z, cc), x)
    for i in far_first(Z):
        for cc in range(2):
            greet(at(y, (z + i) % Z, cc), x)
    for i in far_first(X):
        greet(me, (x + i) % X)
    greet(at(y, z, sib), x)

    bins = spec_ref.shape[3]
    J = bins // 512
    PR = 4 * J
    for copy in inputs:
        copy.wait()
    white = []
    for s in range(2):
        v = spec_ref[s, 0].astype(F32)
        power = jnp.sum(jnp.sum(v * v, axis=1, keepdims=True), axis=0, keepdims=True) * (
            1.0 / (2 * bins)
        )
        white.append(v * lax.rsqrt(power + 1e-05))
    lane = iota((1, 128), 1)
    mask_row = jnp.zeros((1, 128), F32)
    for s in range(2):
        for w in range(X):
            one = mask_ref[s : s + 1, w : w + 1].astype(F32)
            mask_row = jnp.where(lane == s * X + w, one, mask_row)
    packet = jnp.concatenate(
        [
            pair_ref[...].astype(F32), owner_ref[...].astype(F32), mask_row,
            jnp.zeros((12, 128), F32),
        ],
        axis=0,
    ).astype(BF)
    for cc in range(2):
        for h, pk in ((0, pka), (1, pkb)):
            rows = []
            for s in range(2):
                for j in range(J):
                    start = (cc * 2 + h) * (bins // 4) + j * 128
                    rows.append(white[s][:, start : start + 128])
            pk[cc, 0:PR, :] = jnp.concatenate(rows, axis=0).astype(BF)
        pka[cc, PR : PR + 16, :] = packet

    def relayout_perm(size):
        shape = (2 * J * size * 2, size * PR)
        n, k = iota(shape, 0), iota(shape, 1)
        st, rij = mod(n, 2 * size), div(n, 2 * size)
        ri, j = div(rij, J), mod(rij, J)
        return onehot(k == div(st, 2) * PR + mod(st, 2) * 2 * J + j * 2 + ri)

    pl.semaphore_wait(barrier, 2 * (Y - 1) + 2 * (Z - 1) + 1 + X - 1)

    slot_a = y * 2 + c
    slot_b = z * 2 + c

    def send_a(yy, cc):
        pltpu.make_async_remote_copy(
            src_ref=pka.at[cc], dst_ref=p1a.at[slot_a], send_sem=p1a_s, recv_sem=p1a_r,
            device_id=(at(yy, z, cc), x), device_id_type=MESH,
        ).start()

    def send_b(zz, cc):
        pltpu.make_async_remote_copy(
            src_ref=pkb.at[cc], dst_ref=p1b.at[slot_b], send_sem=p1b_s, recv_sem=p1b_r,
            device_id=(at(y, zz, cc), x), device_id_type=MESH,
        ).start()

    for i in far_first(Y):
        for cc in range(2):
            send_a((y + i) % Y, cc)
    send_a(y, sib)
    for i in far_first(Z):
        for cc in range(2):
            send_b((z + i) % Z, cc)
    send_b(z, sib)
    p1a[slot_a] = pka[c]
    p1b[slot_b] = pkb[c]

    tab_copies = [
        pltpu.make_async_copy(table_hbm.at[c, (x + i) % X], table.at[i], tab_sem.at[i])
        for i in range(X)
    ]
    for copy in tab_copies:
        copy.start()

    perm_a[...] = relayout_perm(GA)
    perm_b[...] = relayout_perm(GB)
    share = GA // X
    n, k = iota((4 * share, GA * 16), 0), iota((4 * share, GA * 16), 1)
    perm_l[...] = onehot(k == (x * share + mod(n, share)) * 16 + div(n, share))

    def wait_bytes(ref, sem):
        pltpu.make_async_copy(ref, ref, sem).wait()

    def hop(h, w, direction, dist):
        every, size, pos = ((every_a, Z, z), (every_b, Y, y))[h]
        sign = 1 - 2 * direction
        parent = 2 if dist > 2 else 0
        to = (pos + sign * (dist - parent) + size) % size
        rows = every.shape[2]

        def view(block):
            if 2 * dist == size:
                return every.at[w, block, pl.ds(direction * (rows // 2), rows // 2)]
            return every.at[w, block]

        sent = view((pos - sign * parent + size) % size)
        comes = view((pos - sign * dist + size) % size)
        sems = (ring_s.at[h, w, direction, dist - 1], ring_r.at[h, w, direction, dist - 1])
        dev = (at(y, to, c) if h == 0 else at(to, z, c), x)
        out, arrive = (
            pltpu.make_async_remote_copy(
                src_ref=v, dst_ref=v, send_sem=sems[0], recv_sem=sems[1],
                device_id=dev, device_id_type=MESH,
            )
            for v in (sent, comes)
        )
        return out, arrive

    half_way = (Z // 2, Y // 2)

    def start_direct(h):
        for w in range(W):
            for dist in (2, 1):
                if dist <= half_way[h]:
                    for direction in range(2):
                        hop(h, w, direction, dist)[0].start()

    def forward(h, w):
        if half_way[h] > 2:
            for direction in range(2):
                hop(h, w, direction, 2)[1].wait_recv()
                for dist in range(3, half_way[h] + 1):
                    hop(h, w, direction, dist)[0].start()

    def drain(h, w):
        for dist in range(1, half_way[h] + 1):
            if dist == 2 and half_way[h] > 2:
                continue
            for direction in range(2):
                hop(h, w, direction, dist)[1].wait_recv()

    jw = J // W

    def place(every, pos, perm, group, size):
        block = dot(perm[...], group).astype(BF)
        for w in range(W):
            for ri in range(2):
                for j in range(jw):
                    row = (ri * J + w * jw + j) * 2 * size
                    col = (ri * jw + j) * 128
                    every[w, pos, :, col : col + 128] = block[row : row + 2 * size]

    wait_bytes(p1a.at[pl.ds(0, GA - 1)], p1a_r)

    def lists_x():
        if Z > 1:
            wait_bytes(lists.at[0, pl.ds(0, Z - 1)], l2_r)
        for i in far_first(X):
            pltpu.make_async_remote_copy(
                src_ref=lists.at[x], dst_ref=lists.at[x], send_sem=l3_s, recv_sem=l3_r,
                device_id=(me, (x + i) % X), device_id_type=MESH,
            ).start()

    def prepare():
        n, k = iota((4 * D, 4 * D), 0), iota((4 * D, 4 * D), 1)
        d, q = mod(n, D), div(n, D)
        pos = div(d, 2 * Z) * 2 + mod(d, 2)
        src = (div(pos, share) * Z + mod(div(d, 2), Z)) * (4 * share) + q * share + mod(pos, share)
        perm_s[...] = onehot(k == src)

    def lists_z():
        lists[x, z] = dot(perm_l[...], p1a[:, PR : PR + 16, :].reshape(GA * 16, 128)).astype(BF)
        for i in far_first(Z):
            pltpu.make_async_remote_copy(
                src_ref=lists.at[x, z], dst_ref=lists.at[x, z], send_sem=l2_s, recv_sem=l2_r,
                device_id=(at(y, (z + i) % Z, c), x), device_id_type=MESH,
            ).start()

    lists_z()

    place(every_a, z, perm_a, p1a[:, 0:PR, :].reshape(GA * PR, 128), GA)
    start_direct(0)
    wait_bytes(p1b.at[pl.ds(0, GB - 1)], p1b_r)
    place(every_b, y, perm_b, p1b[...].reshape(GB * PR, 128), GB)
    start_direct(1)
    prepare()
    lists_x()

    forward(0, 0)
    forward(1, 0)
    for w in range(1, W):
        forward(0, w)
        forward(1, w)

    if X > 1:
        wait_bytes(lists.at[pl.ds(0, X - 1)], l3_r)
    sorted_lists = dot(perm_s[...], lists[...].reshape(4 * D, 128))
    first_id = sorted_lists[0:D]
    second_id = sorted_lists[D : 2 * D]
    owner_id = sorted_lists[2 * D : 3 * D]
    mask_rows = sorted_lists[3 * D : 4 * D].astype(BF)
    spread = onehot(div(iota((NST, D), 0), 2) == iota((NST, D), 1))
    lane = iota((NST, 128), 1)
    mine = (div(lane, X) == mod(iota((NST, 128), 0), 2)) & (lane < 2 * X)
    fl, fw = iota((128, 128), 0), iota((128, 128), 1)
    fold = onehot((fl < 2 * X) & (fw < X) & (mod(fl, X) == fw))
    mask_st = dot(jnp.where(mine, dot(spread, mask_rows), 0.0).astype(BF), fold).astype(BF)
    tri = onehot(iota((128, 128), 0) < iota((128, 128), 1))
    ka = iota((2 * D, NST), 1)
    st_a = mod(div(ka, 4), Y) * (4 * Z) + div(ka, 4 * Y) * 4 + mod(ka, 4)
    st_a = st_a.astype(F32)
    st_b = ka.astype(F32)

    def slots_of(which, o):
        match = owner_id == o.astype(F32)
        mf = match.astype(F32)
        before = dot(mf.astype(BF), tri)
        picks = [mf * (before == float(i)).astype(F32) for i in range(2)]
        lane = iota((D, 128), 1)
        for i, p in enumerate(picks):
            first = jnp.sum(p * (first_id + 1.0), axis=1, keepdims=True)
            second = jnp.sum(p * (second_id + 1.0), axis=1, keepdims=True)
            ids[which, pl.ds(i, D, stride=2), :] = jnp.where(lane == 0, first, second) - 1.0
        first, second = ids[which, :, 0:1], ids[which, :, 1:2]
        one_b = [onehot(st_b == first), onehot(st_b == second)]
        one_a = [onehot(st_a == first), onehot(st_a == second)]
        both = dot(one_b[0], mask_st) * dot(one_b[1], mask_st)
        count = jnp.maximum(jnp.sum(both, axis=1, keepdims=True), 1.0)
        here = jnp.where(iota(both.shape, 1) == x, both, 0.0)
        return (one_a, one_b), jnp.sum(here, axis=1, keepdims=True) / count

    slots = [slots_of(0, me - c + sib), slots_of(1, me)]
    for copy in tab_copies:
        copy.wait()

    if X == 4:
        sides = ((2, 1), (3, 0))
    elif X == 2:
        sides = ((1,), (0,))
    else:
        sides = ((0,),)
    quarter = bins // 4 // W

    def stack_of(which, w):
        parts = []
        for h, every in enumerate((every_a, every_b)):
            ones = slots[which][0][h]
            stations = every[w].reshape(NST, 2 * quarter)
            f = dot(ones[0], stations)
            s = dot(ones[1], stations)
            fr, fi = f[:, :quarter], f[:, quarter:]
            sr, si = s[:, :quarter], s[:, quarter:]
            stack = jnp.concatenate([fr * sr + fi * si, fi * sr - fr * si], axis=1)
            high = stack.astype(BF)
            low = (stack - high.astype(F32)).astype(BF)
            parts.append((high, low))
        return parts

    def product(parts, w, side):
        total = None
        for h, (high, low) in enumerate(parts):
            t_high, t_low = (
                jnp.concatenate([table[i, h, w, p] for i in sides[side]], axis=1)
                for p in range(2)
            )
            part = dot(high, t_high) + (dot(high, t_low) + dot(low, t_high))
            total = part if total is None else total + part
        return total

    NS = len(sides)
    wide = 128 * len(sides[0])
    for w in range(W - 1):
        drain(0, w)
        drain(1, w)
        for which in range(2):
            parts = stack_of(which, w)
            for side in range(NS):
                value = product(parts, w, side)
                if w > 0:
                    value = value + acc[which, side]
                acc[which, side] = value
    w = W - 1
    drain(0, w)
    drain(1, w)

    def finish(which, side, parts):
        value = product(parts, w, side)
        if W > 1:
            value = value + acc[which, side]
        return value * slots[which][1]

    def r1_copy(side):
        return pltpu.make_async_remote_copy(
            src_ref=r1_out.at[side], dst_ref=r1_in.at[side], send_sem=r1_s.at[side],
            recv_sem=r1_r.at[side], device_id=(at(y, z, sib), x), device_id_type=MESH,
        )

    def r2_copy(i):
        return pltpu.make_async_remote_copy(
            src_ref=r2_out.at[i], dst_ref=r2_in.at[i - 1], send_sem=r2_s.at[i],
            recv_sem=r2_r.at[i], device_id=(me, (x + i) % X), device_id_type=MESH,
        )

    own_copy = pltpu.make_async_copy(own, own_hbm, own_s)
    parts = stack_of(0, w)
    for side in range(NS):
        r1_out[side] = finish(0, side, parts)
        r1_copy(side).start()
    parts = stack_of(1, w)
    for side in range(NS):
        acc[1, side] = finish(1, side, parts)
    for side in range(NS):
        r1_copy(side).wait_recv()
        for m, i in enumerate(sides[side]):
            piece = acc[1, side, :, m * 128 : (m + 1) * 128] + r1_in[side, :, m * 128 : (m + 1) * 128]
            if i > 0:
                r2_out[i] = piece.astype(BF)
                r2_copy(i).start()
            else:
                own[...] = piece
                own_copy.start()
    wait_bytes(p1a.at[pl.ds(0, GA - 1)], p1a_s)
    wait_bytes(p1b.at[pl.ds(0, GB - 1)], p1b_s)
    if Z > 1:
        wait_bytes(lists.at[0, pl.ds(0, Z - 1)], l2_s)
    if X > 1:
        wait_bytes(lists.at[pl.ds(0, X - 1)], l3_s)
    for h in range(2):
        for w in range(W):
            for direction in range(2):
                for dist in range(1, half_way[h] + 1):
                    hop(h, w, direction, dist)[0].wait_send()
    for side in range(NS):
        r1_copy(side).wait_send()
    for i in range(1, X):
        r2_copy(i).wait_send()
    own_copy.wait()
    for i in range(1, X):
        r2_copy(i).wait_recv()


def body(dims, spectra, masks, pairs, owners):
    Y, Z, X = dims
    bins = spectra.shape[3]
    lags = 128 * X
    D = 2 * Y * Z
    J = bins // 512
    PR = 4 * J
    W = WAVES
    table = jnp.asarray(lag_tables(bins, lags))
    sides = 2 if X > 1 else 1
    wide = lags // sides
    dma = pltpu.SemaphoreType.DMA
    own, others = pl.pallas_call(
        functools.partial(kernel, Y, Z, X),
        out_shape=(
            jax.ShapeDtypeStruct((2 * D, 128), F32),
            jax.ShapeDtypeStruct((max(X - 1, 1), 2 * D, 128), BF),
        ),
        in_specs=[pl.BlockSpec(memory_space=pl.ANY)] * 5,
        out_specs=[pl.BlockSpec(memory_space=pl.ANY)] * 2,
        scratch_shapes=[
            pltpu.VMEM(spectra.shape, BF),
            pltpu.VMEM(masks.shape, I32),
            pltpu.VMEM((2, 128), I32),
            pltpu.VMEM((1, 128), I32),
            pltpu.VMEM(table.shape[1:], BF),
            pltpu.VMEM((8 * J * Y, 2 * Y * PR), BF),
            pltpu.VMEM((8 * J * Z, 2 * Z * PR), BF),
            pltpu.VMEM((4 * (2 * Y // X), 2 * Y * 16), BF),
            pltpu.VMEM((4 * D, 4 * D), BF),
            pltpu.VMEM((2, PR + 16, 128), BF),
            pltpu.VMEM((2, PR, 128), BF),
            pltpu.VMEM((2 * Y, PR + 16, 128), BF),
            pltpu.VMEM((2 * Z, PR, 128), BF),
            pltpu.VMEM((W, Z, 4 * Y, 2 * J * 128 // W), BF),
            pltpu.VMEM((W, Y, 4 * Z, 2 * J * 128 // W), BF),
            pltpu.VMEM((X, Z, 4 * (2 * Y // X), 128), BF),
            pltpu.VMEM((2, sides, 2 * D, wide), F32),
            pltpu.VMEM((sides, 2 * D, wide), F32),
            pltpu.VMEM((sides, 2 * D, wide), F32),
            pltpu.VMEM((X, 2 * D, 128), BF),
            pltpu.VMEM((2 * D, 128), F32),
            pltpu.VMEM((2, 2 * D, 128), F32),
            dma((4,)), dma((X,)), dma, dma, dma, dma,
            dma((2, W, 2, max(Y, Z) // 2)),
            dma((2, W, 2, max(Y, Z) // 2)),
            dma, dma, dma, dma,
            dma((sides,)), dma((sides,)), dma((X,)), dma((X,)), dma,
        ],
        compiler_params=pltpu.CompilerParams(
            collective_id=0, has_side_effects=True, vmem_limit_bytes=63 * 1024 * 1024
        ),
    )(spectra, masks, pairs.T, owners.T, table)
    for i in range(X - 1):
        own = own + others[i].astype(F32)
    return own


def dims_of(mesh):
    sta, win = mesh.shape["sta"], mesh.shape["win"]
    side = math.isqrt(sta // 2)
    return side, sta // 2 // side, win


def solution(mesh):
    placed = (P("sta", "win", None, None), P("sta", None), P("sta", None), P("sta", None))
    return jax.shard_map(
        functools.partial(body, dims_of(mesh)),
        mesh=mesh, in_specs=placed, out_specs=P("sta", "win"), check_vma=False,
    )
```

```python
import functools
import math

import jax
import jax.numpy as jnp
import ml_dtypes
import numpy as np
from jax import lax
from jax.experimental import pallas as pl
from jax.experimental.pallas import tpu as pltpu
from jax.sharding import PartitionSpec as P

FIRST_BIN = 360
SAMPLES = 180000
WAVES = 2
MESH = pl.DeviceIdType.MESH
BF = jnp.bfloat16
F32 = jnp.float32
I32 = jnp.int32


def lag_tables(bins, lags):
    freq = np.arange(bins, dtype=np.int64)[:, None] + FIRST_BIN
    lag = np.arange(lags, dtype=np.int64)[None, :] - lags // 2
    angle = (freq * lag % SAMPLES).astype(np.float64) * (2.0 * math.pi / SAMPLES)
    scale = bins ** (-0.5)
    both = np.stack([np.cos(angle) * scale, -np.sin(angle) * scale]).astype(np.float32)
    both = both.reshape(2, 2, 2, WAVES, bins // 4 // WAVES, lags // 128, 128)
    both = both.transpose(1, 5, 2, 3, 0, 4, 6)
    both = both.reshape(2, lags // 128, 2, WAVES, bins // 2 // WAVES, 128)
    high = both.astype(ml_dtypes.bfloat16)
    low = (both - high.astype(np.float32)).astype(ml_dtypes.bfloat16)
    return np.stack([high, low], axis=4)


def iota(shape, dim):
    return lax.broadcasted_iota(I32, shape, dim)


def onehot(cond):
    return cond.astype(F32).astype(BF)


def dot(a, b):
    return jnp.dot(a, b, preferred_element_type=F32)


def div(a, n):
    return lax.shift_right_logical(a, jnp.full_like(a, n.bit_length() - 1))


def mod(a, n):
    return a & (n - 1)


def kernel(
    Y, Z, X,
    spec_hbm, mask_hbm, pair_hbm, owner_hbm, table_hbm, own_hbm, r2_in,
    spec_ref, mask_ref, pair_ref, owner_ref, table, perm_a, perm_b, perm_l, perm_s,
    pka, pkb, p1a, p1b, every_a, every_b, lists, acc, r1_out, r1_in, r2_out, own, ids,
    in_sem, tab_sem, p1a_s, p1a_r, p1b_s, p1b_r, ring_s, ring_r, l2_s, l2_r, l3_s, l3_r,
    r1_s, r1_r, r2_s, r2_r, own_s,
):
    D = 2 * Y * Z
    NST = 2 * D
    GA, GB = 2 * Y, 2 * Z
    W = WAVES
    me = lax.axis_index("sta")
    x = lax.axis_index("win")
    y = me // (2 * Z)
    z = (me // 2) % Z
    c = me % 2
    sib = 1 - c

    def at(yy, zz, cc):
        return (yy * Z + zz) * 2 + cc

    inputs = [
        pltpu.make_async_copy(src, dst, in_sem.at[i])
        for i, (src, dst) in enumerate(
            ((spec_hbm, spec_ref), (pair_hbm, pair_ref), (owner_hbm, owner_ref), (mask_hbm, mask_ref))
        )
    ]
    for copy in inputs:
        copy.start()

    barrier = pltpu.get_barrier_semaphore()

    def greet(sta, win):
        pl.semaphore_signal(barrier, inc=1, device_id=(sta, win), device_id_type=MESH)

    def far_first(size):
        return sorted(range(1, size), key=lambda i: -min(i, size - i))

    for i in far_first(Y):
        for cc in range(2):
            greet(at((y + i) % Y, z, cc), x)
    for i in far_first(Z):
        for cc in range(2):
            greet(at(y, (z + i) % Z, cc), x)
    for i in far_first(X):
        greet(me, (x + i) % X)
    greet(at(y, z, sib), x)

    bins = spec_ref.shape[3]
    J = bins // 512
    PR = 4 * J
    for copy in inputs:
        copy.wait()
    white = []
    for s in range(2):
        v = spec_ref[s, 0].astype(F32)
        power = jnp.sum(jnp.sum(v * v, axis=1, keepdims=True), axis=0, keepdims=True) * (
            1.0 / (2 * bins)
        )
        white.append(v * lax.rsqrt(power + 1e-05))
    lane = iota((1, 128), 1)
    mask_row = jnp.zeros((1, 128), F32)
    for s in range(2):
        for w in range(X):
            one = mask_ref[s : s + 1, w : w + 1].astype(F32)
            mask_row = jnp.where(lane == s * X + w, one, mask_row)
    packet = jnp.concatenate(
        [
            pair_ref[...].astype(F32), owner_ref[...].astype(F32), mask_row,
            jnp.zeros((12, 128), F32),
        ],
        axis=0,
    ).astype(BF)
    for cc in range(2):
        for h, pk in ((0, pka), (1, pkb)):
            rows = []
            for s in range(2):
                for j in range(J):
                    start = (cc * 2 + h) * (bins // 4) + j * 128
                    rows.append(white[s][:, start : start + 128])
            pk[cc, 0:PR, :] = jnp.concatenate(rows, axis=0).astype(BF)
        pka[cc, PR : PR + 16, :] = packet

    def relayout_perm(size):
        shape = (2 * J * size * 2, size * PR)
        n, k = iota(shape, 0), iota(shape, 1)
        st, rij = mod(n, 2 * size), div(n, 2 * size)
        ri, j = div(rij, J), mod(rij, J)
        return onehot(k == div(st, 2) * PR + mod(st, 2) * 2 * J + j * 2 + ri)

    pl.semaphore_wait(barrier, 2 * (Y - 1) + 2 * (Z - 1) + 1 + X - 1)

    slot_a = y * 2 + c
    slot_b = z * 2 + c

    def send_a(yy, cc):
        pltpu.make_async_remote_copy(
            src_ref=pka.at[cc], dst_ref=p1a.at[slot_a], send_sem=p1a_s, recv_sem=p1a_r,
            device_id=(at(yy, z, cc), x), device_id_type=MESH,
        ).start()

    def send_b(zz, cc):
        pltpu.make_async_remote_copy(
            src_ref=pkb.at[cc], dst_ref=p1b.at[slot_b], send_sem=p1b_s, recv_sem=p1b_r,
            device_id=(at(y, zz, cc), x), device_id_type=MESH,
        ).start()

    for i in far_first(Y):
        for cc in range(2):
            send_a((y + i) % Y, cc)
    send_a(y, sib)
    for i in far_first(Z):
        for cc in range(2):
            send_b((z + i) % Z, cc)
    send_b(z, sib)
    p1a[slot_a] = pka[c]
    p1b[slot_b] = pkb[c]

    tab_copies = [
        pltpu.make_async_copy(table_hbm.at[c, (x + i) % X], table.at[i], tab_sem.at[i])
        for i in range(X)
    ]
    for copy in tab_copies:
        copy.start()

    perm_a[...] = relayout_perm(GA)
    perm_b[...] = relayout_perm(GB)
    share = GA // X
    n, k = iota((4 * share, GA * 16), 0), iota((4 * share, GA * 16), 1)
    perm_l[...] = onehot(k == (x * share + mod(n, share)) * 16 + div(n, share))

    def wait_bytes(ref, sem):
        pltpu.make_async_copy(ref, ref, sem).wait()

    def hop(h, w, direction, dist):
        every, size, pos = ((every_a, Z, z), (every_b, Y, y))[h]
        sign = 1 - 2 * direction
        parent = 2 if dist > 2 else 0
        to = (pos + sign * (dist - parent) + size) % size
        rows = every.shape[2]

        def view(block):
            if 2 * dist == size:
                return every.at[w, block, pl.ds(direction * (rows // 2), rows // 2)]
            return every.at[w, block]

        sent = view((pos - sign * parent + size) % size)
        comes = view((pos - sign * dist + size) % size)
        sems = (ring_s.at[h, w, direction, dist - 1], ring_r.at[h, w, direction, dist - 1])
        dev = (at(y, to, c) if h == 0 else at(to, z, c), x)
        out, arrive = (
            pltpu.make_async_remote_copy(
                src_ref=v, dst_ref=v, send_sem=sems[0], recv_sem=sems[1],
                device_id=dev, device_id_type=MESH,
            )
            for v in (sent, comes)
        )
        return out, arrive

    half_way = (Z // 2, Y // 2)

    def start_direct(h):
        for w in range(W):
            for dist in (2, 1):
                if dist <= half_way[h]:
                    for direction in range(2):
                        hop(h, w, direction, dist)[0].start()

    def forward(h, w):
        if half_way[h] > 2:
            for direction in range(2):
                hop(h, w, direction, 2)[1].wait_recv()
                for dist in range(3, half_way[h] + 1):
                    hop(h, w, direction, dist)[0].start()

    def drain(h, w):
        for dist in range(1, half_way[h] + 1):
            if dist == 2 and half_way[h] > 2:
                continue
            for direction in range(2):
                hop(h, w, direction, dist)[1].wait_recv()

    jw = J // W

    def place(every, pos, perm, group, size):
        block = dot(perm[...], group).astype(BF)
        for w in range(W):
            for ri in range(2):
                for j in range(jw):
                    row = (ri * J + w * jw + j) * 2 * size
                    col = (ri * jw + j) * 128
                    every[w, pos, :, col : col + 128] = block[row : row + 2 * size]

    n, k = iota((4 * D, 4 * D), 0), iota((4 * D, 4 * D), 1)
    d, q = mod(n, D), div(n, D)
    pos = div(d, 2 * Z) * 2 + mod(d, 2)
    src = (div(pos, share) * Z + mod(div(d, 2), Z)) * (4 * share) + q * share + mod(pos, share)
    perm_s[...] = onehot(k == src)

    wait_bytes(p1a.at[pl.ds(0, GA - 1)], p1a_r)

    def lists_x():
        if Z > 1:
            wait_bytes(lists.at[0, pl.ds(0, Z - 1)], l2_r)
        for i in far_first(X):
            pltpu.make_async_remote_copy(
                src_ref=lists.at[x], dst_ref=lists.at[x], send_sem=l3_s, recv_sem=l3_r,
                device_id=(me, (x + i) % X), device_id_type=MESH,
            ).start()

    def lists_z():
        lists[x, z] = dot(perm_l[...], p1a[:, PR : PR + 16, :].reshape(GA * 16, 128)).astype(BF)
        for i in far_first(Z):
            pltpu.make_async_remote_copy(
                src_ref=lists.at[x, z], dst_ref=lists.at[x, z], send_sem=l2_s, recv_sem=l2_r,
                device_id=(at(y, (z + i) % Z, c), x), device_id_type=MESH,
            ).start()

    lists_z()

    place(every_a, z, perm_a, p1a[:, 0:PR, :].reshape(GA * PR, 128), GA)
    start_direct(0)
    wait_bytes(p1b.at[pl.ds(0, GB - 1)], p1b_r)
    place(every_b, y, perm_b, p1b[...].reshape(GB * PR, 128), GB)
    start_direct(1)
    lists_x()

    forward(0, 0)
    forward(1, 0)
    for w in range(1, W):
        forward(0, w)
        forward(1, w)

    if X > 1:
        wait_bytes(lists.at[pl.ds(0, X - 1)], l3_r)
    sorted_lists = dot(perm_s[...], lists[...].reshape(4 * D, 128))
    first_id = sorted_lists[0:D]
    second_id = sorted_lists[D : 2 * D]
    owner_id = sorted_lists[2 * D : 3 * D]
    mask_rows = sorted_lists[3 * D : 4 * D].astype(BF)
    spread = onehot(div(iota((NST, D), 0), 2) == iota((NST, D), 1))
    lane = iota((NST, 128), 1)
    mine = (div(lane, X) == mod(iota((NST, 128), 0), 2)) & (lane < 2 * X)
    fl, fw = iota((128, 128), 0), iota((128, 128), 1)
    fold = onehot((fl < 2 * X) & (fw < X) & (mod(fl, X) == fw))
    mask_st = dot(jnp.where(mine, dot(spread, mask_rows), 0.0).astype(BF), fold).astype(BF)
    tri = onehot(iota((128, 128), 0) < iota((128, 128), 1))
    ka = iota((2 * D, NST), 1)
    st_a = mod(div(ka, 4), Y) * (4 * Z) + div(ka, 4 * Y) * 4 + mod(ka, 4)
    st_a = st_a.astype(F32)
    st_b = ka.astype(F32)

    def slots_of(which, o):
        match = owner_id == o.astype(F32)
        mf = match.astype(F32)
        before = dot(mf.astype(BF), tri)
        picks = [mf * (before == float(i)).astype(F32) for i in range(2)]
        lane = iota((D, 128), 1)
        for i, p in enumerate(picks):
            first = jnp.sum(p * (first_id + 1.0), axis=1, keepdims=True)
            second = jnp.sum(p * (second_id + 1.0), axis=1, keepdims=True)
            ids[which, pl.ds(i, D, stride=2), :] = jnp.where(lane == 0, first, second) - 1.0
        first, second = ids[which, :, 0:1], ids[which, :, 1:2]
        one_b = [onehot(st_b == first), onehot(st_b == second)]
        one_a = [onehot(st_a == first), onehot(st_a == second)]
        both = dot(one_b[0], mask_st) * dot(one_b[1], mask_st)
        count = jnp.maximum(jnp.sum(both, axis=1, keepdims=True), 1.0)
        here = jnp.where(iota(both.shape, 1) == x, both, 0.0)
        return (one_a, one_b), jnp.sum(here, axis=1, keepdims=True) / count

    slots = [slots_of(0, me - c + sib), slots_of(1, me)]
    for copy in tab_copies:
        copy.wait()

    if X == 4:
        sides = ((2, 1), (3, 0))
    elif X == 2:
        sides = ((1,), (0,))
    else:
        sides = ((0,),)
    quarter = bins // 4 // W

    def stack_of(which, w):
        parts = []
        for h, every in enumerate((every_a, every_b)):
            firsts = [slots[g][0][h][0] for g in which]
            seconds = [slots[g][0][h][1] for g in which]
            both = dot(jnp.concatenate(firsts + seconds, axis=0), every[w].reshape(NST, 2 * quarter))
            rows = both.shape[0] // 2
            f, s = both[:rows], both[rows:]
            fr, fi = f[:, :quarter], f[:, quarter:]
            sr, si = s[:, :quarter], s[:, quarter:]
            stack = jnp.concatenate([fr * sr + fi * si, fi * sr - fr * si], axis=1)
            high = stack.astype(BF)
            low = (stack - high.astype(F32)).astype(BF)
            parts.append((high, low))
        return parts

    def product(parts, w, side):
        total = None
        for h, (high, low) in enumerate(parts):
            t_high, t_low = (
                jnp.concatenate([table[i, h, w, p] for i in sides[side]], axis=1)
                for p in range(2)
            )
            part = dot(high, t_high) + (dot(high, t_low) + dot(low, t_high))
            total = part if total is None else total + part
        return total

    NS = len(sides)
    wide = 128 * len(sides[0])
    for w in range(W - 1):
        drain(0, w)
        drain(1, w)
        parts = stack_of((0, 1), w)
        for side in range(NS):
            value = product(parts, w, side)
            for which in range(2):
                piece = value[which * 2 * D : (which + 1) * 2 * D]
                if w > 0:
                    piece = piece + acc[which, side]
                acc[which, side] = piece
    w = W - 1
    drain(0, w)
    drain(1, w)

    def finish(which, side, parts):
        value = product(parts, w, side)
        if W > 1:
            value = value + acc[which, side]
        return value * slots[which][1]

    def r1_copy(side):
        return pltpu.make_async_remote_copy(
            src_ref=r1_out.at[side], dst_ref=r1_in.at[side], send_sem=r1_s.at[side],
            recv_sem=r1_r.at[side], device_id=(at(y, z, sib), x), device_id_type=MESH,
        )

    def r2_copy(i):
        return pltpu.make_async_remote_copy(
            src_ref=r2_out.at[i], dst_ref=r2_in.at[i - 1], send_sem=r2_s.at[i],
            recv_sem=r2_r.at[i], device_id=(me, (x + i) % X), device_id_type=MESH,
        )

    own_copy = pltpu.make_async_copy(own, own_hbm, own_s)
    parts = stack_of((0,), w)
    for side in range(NS):
        r1_out[side] = finish(0, side, parts)
        r1_copy(side).start()
    parts = stack_of((1,), w)
    for side in range(NS):
        acc[1, side] = finish(1, side, parts)
        r1_copy(side).wait_recv()
        for m, i in enumerate(sides[side]):
            piece = acc[1, side, :, m * 128 : (m + 1) * 128] + r1_in[side, :, m * 128 : (m + 1) * 128]
            if i > 0:
                r2_out[i] = piece.astype(BF)
                r2_copy(i).start()
            else:
                own[...] = piece
                own_copy.start()
    wait_bytes(p1a.at[pl.ds(0, GA - 1)], p1a_s)
    wait_bytes(p1b.at[pl.ds(0, GB - 1)], p1b_s)
    if Z > 1:
        wait_bytes(lists.at[0, pl.ds(0, Z - 1)], l2_s)
    if X > 1:
        wait_bytes(lists.at[pl.ds(0, X - 1)], l3_s)
    for h in range(2):
        for w in range(W):
            for direction in range(2):
                for dist in range(1, half_way[h] + 1):
                    hop(h, w, direction, dist)[0].wait_send()
    for side in range(NS):
        r1_copy(side).wait_send()
    for i in range(1, X):
        r2_copy(i).wait_send()
    own_copy.wait()
    for i in range(1, X):
        r2_copy(i).wait_recv()


def body(dims, spectra, masks, pairs, owners):
    Y, Z, X = dims
    bins = spectra.shape[3]
    lags = 128 * X
    D = 2 * Y * Z
    J = bins // 512
    PR = 4 * J
    W = WAVES
    table = jnp.asarray(lag_tables(bins, lags))
    sides = 2 if X > 1 else 1
    wide = lags // sides
    dma = pltpu.SemaphoreType.DMA
    own, others = pl.pallas_call(
        functools.partial(kernel, Y, Z, X),
        out_shape=(
            jax.ShapeDtypeStruct((2 * D, 128), F32),
            jax.ShapeDtypeStruct((max(X - 1, 1), 2 * D, 128), BF),
        ),
        in_specs=[pl.BlockSpec(memory_space=pl.ANY)] * 5,
        out_specs=[pl.BlockSpec(memory_space=pl.ANY)] * 2,
        scratch_shapes=[
            pltpu.VMEM(spectra.shape, BF),
            pltpu.VMEM(masks.shape, I32),
            pltpu.VMEM((2, 128), I32),
            pltpu.VMEM((1, 128), I32),
            pltpu.VMEM(table.shape[1:], BF),
            pltpu.VMEM((8 * J * Y, 2 * Y * PR), BF),
            pltpu.VMEM((8 * J * Z, 2 * Z * PR), BF),
            pltpu.VMEM((4 * (2 * Y // X), 2 * Y * 16), BF),
            pltpu.VMEM((4 * D, 4 * D), BF),
            pltpu.VMEM((2, PR + 16, 128), BF),
            pltpu.VMEM((2, PR, 128), BF),
            pltpu.VMEM((2 * Y, PR + 16, 128), BF),
            pltpu.VMEM((2 * Z, PR, 128), BF),
            pltpu.VMEM((W, Z, 4 * Y, 2 * J * 128 // W), BF),
            pltpu.VMEM((W, Y, 4 * Z, 2 * J * 128 // W), BF),
            pltpu.VMEM((X, Z, 4 * (2 * Y // X), 128), BF),
            pltpu.VMEM((2, sides, 2 * D, wide), F32),
            pltpu.VMEM((sides, 2 * D, wide), F32),
            pltpu.VMEM((sides, 2 * D, wide), F32),
            pltpu.VMEM((X, 2 * D, 128), BF),
            pltpu.VMEM((2 * D, 128), F32),
            pltpu.VMEM((2, 2 * D, 128), F32),
            dma((4,)), dma((X,)), dma, dma, dma, dma,
            dma((2, W, 2, max(Y, Z) // 2)),
            dma((2, W, 2, max(Y, Z) // 2)),
            dma, dma, dma, dma,
            dma((sides,)), dma((sides,)), dma((X,)), dma((X,)), dma,
        ],
        compiler_params=pltpu.CompilerParams(
            collective_id=0, has_side_effects=True, vmem_limit_bytes=63 * 1024 * 1024
        ),
    )(spectra, masks, pairs.T, owners.T, table)
    for i in range(X - 1):
        own = own + others[i].astype(F32)
    return own


def dims_of(mesh):
    sta, win = mesh.shape["sta"], mesh.shape["win"]
    side = math.isqrt(sta // 2)
    return side, sta // 2 // side, win


def solution(mesh):
    placed = (P("sta", "win", None, None), P("sta", None), P("sta", None), P("sta", None))
    return jax.shard_map(
        functools.partial(body, dims_of(mesh)),
        mesh=mesh, in_specs=placed, out_specs=P("sta", "win"), check_vma=False,
    )
```
